512 devices in a mesh: prefix: 32 (over y_lo, z, core), resp: 16 (over x, y_hi).
Axes of the slice: x: 4, y: 8 (y_hi: 4, y_lo: 2; y = y_hi * 2 + y_lo), z: 8, core: 2. Of those that a mesh axis runs over, the one named last changes fastest.
Arguments:
- prefix_q: bfloat16 [4096, 8192], P('prefix', 'resp'), may hold values from -0.1796875 to 0.1796875
- prefix_k: bfloat16 [4096, 8192], P('prefix', 'resp'), may hold values from -0.08984375 to 0.08984375
- prefix_v: bfloat16 [4096, 8192], P('prefix', 'resp'), may hold values from -6 to 6
- prefix_dout: bfloat16 [4096, 8192], P('prefix', 'resp'), may hold values from -3 to 3
- resp_q: bfloat16 [16, 256, 8192], P('resp', None, 'prefix'), may hold values from -0.1796875 to 0.1796875
- resp_k: bfloat16 [16, 256, 8192], P('resp', None, 'prefix'), may hold values from -0.1796875 to 0.1796875
- resp_v: bfloat16 [16, 256, 8192], P('resp', None, 'prefix'), may hold values from -6 to 6
- resp_dout: bfloat16 [16, 256, 8192], P('resp', None, 'prefix'), may hold values from -0.75 to 0.75
- resp_lengths: int32 [16], P('resp'), may hold values from 128 to 256, as said below
- decay_exps: int32 [64], replicated, may hold values from 5120 to 16383
Outputs:
- prefix_dq: bfloat16 [4096, 8192], P('prefix', 'resp')
- prefix_dk: bfloat16 [4096, 8192], P('prefix', 'resp')
- prefix_dv: bfloat16 [4096, 8192], P('prefix', 'resp')
- resp_dq: bfloat16 [16, 256, 8192], P('resp', None, 'prefix')
- resp_dk: bfloat16 [16, 256, 8192], P('resp', None, 'prefix')
- resp_dv: bfloat16 [16, 256, 8192], P('resp', None, 'prefix')
The draws below stay inside these ranges and needn't reach their ends.
Inputs may be any that keep to these rules, and one draw needn't show every extreme that they name: `resp_lengths`: each length is a multiple of 128; some response has exactly 256 tokens.
All inputs are finite; a program needn't handle non-finite values.
Results may differ from the reference program's by a relative error of at most 0.0057.
Values may be sent and summed in bfloat16 or wider, within the bound.
No kernel may reach another device: no remote copies, remote signals or barrier semaphores. Data moves between devices by JAX's collectives and lax.ppermute only.
A program may use at most 128 MiB of HBM per device.

```python
import jax
import jax.numpy as jnp
from jax import lax

D = 128
HEADS = 64
STRETCH = 128
TRACT = 128
RESP_LEN = 256
PLEN = 4096
RESPONSES = 16
N_PREFIX = 32


def draw_resp_lengths(key, part):
    key = jax.random.fold_in(key, 7)
    key_one, key_two = jax.random.split(key)
    blocks = RESP_LEN // 128
    counts = jax.random.randint(key_one, (RESPONSES,), 1, blocks + 1)
    longest = jax.random.randint(key_two, (), 0, RESPONSES)
    counts = jnp.where(jnp.arange(RESPONSES) == longest, blocks, counts)
    return (counts * 128).astype(jnp.int32)


def touch_ends(values, rng, least, high):
    longest = values.shape.index(max(values.shape))
    spots = []
    for shift in (0, 1):
        where = [jax.random.randint(jax.random.fold_in(rng, axis), (), 0, length) for axis, length in enumerate(values.shape)]
        where[longest] = (where[longest] + shift) % values.shape[longest]
        spots.append(tuple(where))
    return values.at[spots[0]].set(least).at[spots[1]].set(high)


def steps_of(own_key, extent, shards, least, largest):
    factor_of, own = 1.0, jax.random.fold_in(own_key, 6)
    for axis_at, parts in shards:
        heights = jnp.exp(jax.random.uniform(jax.random.fold_in(own, axis_at), (parts,), jnp.float32, least / len(shards), largest / len(shards)))
        factor_of = factor_of * jnp.repeat(heights, extent[axis_at] // parts).reshape([-1 if axis == axis_at else 1 for axis in range(len(extent))])
    return factor_of


def gaussian(own_key, shape, width, reach, cuts=(), kind=jnp.bfloat16):
    result = width * jax.random.normal(own_key, shape, jnp.float32)
    if cuts:
        result = result * steps_of(own_key, shape, cuts, -0.22, 0.18)
    return jnp.clip(result, -reach, reach).astype(kind)


def setup_inputs(seed: int = 0) -> dict:
    keys = jax.random.split(jax.random.key(seed), 11)
    return {
        "prefix_q": gaussian(keys[0], (PLEN, HEADS * D), 0.03, 0.1796875, ((0, 32), (1, 16))),
        "prefix_k": gaussian(keys[1], (PLEN, HEADS * D), 0.015, 0.08984375, ((0, 32), (1, 16))),
        "prefix_v": gaussian(keys[2], (PLEN, HEADS * D), 1.0, 6.0, ((0, 32), (1, 16))),
        "prefix_dout": gaussian(keys[3], (PLEN, HEADS * D), 0.5, 3.0, ((0, 32), (1, 16))),
        "resp_q": gaussian(keys[4], (RESPONSES, RESP_LEN, HEADS * D), 0.03, 0.1796875, ((0, 16), (2, 32))),
        "resp_k": gaussian(keys[5], (RESPONSES, RESP_LEN, HEADS * D), 0.03, 0.1796875, ((0, 16), (2, 32))),
        "resp_v": gaussian(keys[6], (RESPONSES, RESP_LEN, HEADS * D), 1.0, 6.0, ((0, 16), (2, 32))),
        "resp_dout": gaussian(keys[7], (RESPONSES, RESP_LEN, HEADS * D), 0.125, 0.75, ((0, 16), (2, 32))),
        "resp_lengths": draw_resp_lengths(jax.random.fold_in(keys[10], 71), 0),
        "decay_exps": touch_ends(jax.random.randint(keys[9], (HEADS,), 5120, 16384), jax.random.fold_in(keys[9], 1), 5120, 16383).astype(jnp.int32),
    }


def decay_matrix(decay_rates, count):
    places = jnp.arange(count)
    offsets = (places[:, None] - places[None, :]).astype(jnp.float32)
    return jnp.where(offsets[None] >= 0.0, jnp.exp(-decay_rates[:, None, None] * jnp.maximum(offsets, 0.0)[None]), 0.0)


def local_grads(queries, keys_in, values, grad_out, decay_rates):
    decay_mask = decay_matrix(decay_rates, queries.shape[0])
    query_f = queries.astype(jnp.float32)
    key_f = keys_in.astype(jnp.float32)
    value_f = values.astype(jnp.float32)
    grad_f = grad_out.astype(jnp.float32)
    scores = jnp.einsum("thd,shd->hts", query_f, key_f)
    weights = (scores * decay_mask).astype(jnp.bfloat16).astype(jnp.float32)
    dscores = (jnp.einsum("thd,shd->hts", grad_f, value_f) * decay_mask).astype(jnp.bfloat16).astype(jnp.float32)
    grad_q = jnp.einsum("hts,shd->thd", dscores, key_f)
    grad_k = jnp.einsum("hts,thd->shd", dscores, query_f)
    grad_v = jnp.einsum("hts,thd->shd", weights, grad_f)
    return grad_q, grad_k, grad_v


def weighted_outer(left, weight, right):
    scaled = (left.astype(jnp.float32) * weight[..., None]).astype(jnp.bfloat16).astype(jnp.float32)
    return jnp.einsum("...thd,...the->...hde", scaled, right.astype(jnp.float32))


def reference(prefix_q, prefix_k, prefix_v, prefix_dout, resp_q, resp_k, resp_v, resp_dout, resp_lengths, decay_exps):
    decay_rates = jnp.exp2(-decay_exps.astype(jnp.float32) / 1024.0)
    tract_shape = (N_PREFIX, TRACT, HEADS, D)
    pre_q = prefix_q.reshape(tract_shape)
    pre_k = prefix_k.reshape(tract_shape)
    pre_v = prefix_v.reshape(tract_shape)
    pre_g = prefix_dout.reshape(tract_shape)
    grad_q, grad_k, grad_v = jax.vmap(local_grads, in_axes=(0, 0, 0, 0, None))(pre_q, pre_k, pre_v, pre_g, decay_rates)
    places = jnp.arange(TRACT).astype(jnp.float32)
    key_weight = jnp.exp(-decay_rates[None, :] * (TRACT - 1.0 - places)[:, None])
    query_weight = jnp.exp(-decay_rates[None, :] * places[:, None])
    tract_kv = weighted_outer(pre_k, key_weight[None], pre_v)
    tract_qd = weighted_outer(pre_q, query_weight[None], pre_g)
    tract_decay = jnp.exp(-decay_rates * TRACT)

    def forward(state, term):
        return state * tract_decay[:, None, None] + term, state

    last_state, states_in = lax.scan(forward, jnp.zeros((HEADS, D, D), jnp.float32), tract_kv)
    start_state = last_state.astype(jnp.bfloat16).astype(jnp.float32)

    inside = jnp.arange(RESP_LEN)[None, :] < resp_lengths[:, None]
    masked = jnp.where(inside[:, :, None], resp_dout, jnp.zeros_like(resp_dout))
    resp_shape = (RESPONSES, RESP_LEN, HEADS, D)
    block_count = RESP_LEN // STRETCH
    block_shape = (block_count, STRETCH, HEADS, D)
    resp_places = jnp.arange(RESP_LEN).astype(jnp.float32)
    resp_qweight = jnp.exp(-decay_rates[None, :] * resp_places[:, None])
    resp_sweight = jnp.exp(-decay_rates[None, :] * (resp_places + 1.0)[:, None])
    inner_pos = jnp.arange(STRETCH).astype(jnp.float32)
    block_kweight = jnp.exp(-decay_rates[None, :] * (STRETCH - 1.0 - inner_pos)[:, None])
    block_qweight = jnp.exp(-decay_rates[None, :] * inner_pos[:, None])
    block_inw = jnp.exp(-decay_rates[None, :] * (inner_pos + 1.0)[:, None])[None, :, :, None]
    block_outw = jnp.exp(-decay_rates[None, :] * (STRETCH - inner_pos)[:, None])[None, :, :, None]
    block_decay = jnp.exp(-decay_rates * STRETCH)

    def advance(state, term):
        return state * block_decay[:, None, None] + term, state

    def one_response(inputs):
        queries, keys_in, values, grad_out = inputs
        blk_q = queries.reshape(block_shape)
        blk_k = keys_in.reshape(block_shape)
        blk_v = values.reshape(block_shape)
        blk_g = grad_out.reshape(block_shape)
        local_q, local_k, local_v = jax.vmap(local_grads, in_axes=(0, 0, 0, 0, None))(blk_q, blk_k, blk_v, blk_g, decay_rates)
        blk_kv = weighted_outer(blk_k, block_kweight[None], blk_v)
        blk_qd = weighted_outer(blk_q, block_qweight[None], blk_g)
        zeros = jnp.zeros((HEADS, D, D), jnp.float32)
        unused_a, resp_in = lax.scan(advance, zeros, blk_kv)
        unused_b, resp_out = lax.scan(advance, zeros, blk_qd, reverse=True)
        in_b = resp_in.astype(jnp.bfloat16).astype(jnp.float32)
        out_b = resp_out.astype(jnp.bfloat16).astype(jnp.float32)
        dq_blocks = local_q + jnp.einsum("pthe,phde->pthd", blk_g.astype(jnp.float32), in_b) * block_inw
        dk_blocks = local_k + jnp.einsum("pthe,phde->pthd", blk_v.astype(jnp.float32), out_b) * block_outw
        dv_blocks = local_v + jnp.einsum("pthd,phde->pthe", blk_k.astype(jnp.float32), out_b) * block_outw
        from_state = jnp.einsum("the,hde->thd", grad_out.astype(jnp.float32), start_state) * resp_sweight[:, :, None]
        carried = weighted_outer(queries, resp_qweight, grad_out)
        whole = (RESP_LEN, HEADS, D)
        return (dq_blocks.reshape(whole) + from_state).astype(jnp.bfloat16), dk_blocks.reshape(whole).astype(jnp.bfloat16), dv_blocks.reshape(whole).astype(jnp.bfloat16), carried

    resp_dq, resp_dk, resp_dv, carried = lax.map(one_response, (resp_q.reshape(resp_shape), resp_k.reshape(resp_shape), resp_v.reshape(resp_shape), masked.reshape(resp_shape)))
    carried_total = jnp.sum(carried, axis=0)

    def backward(state, term):
        return state * tract_decay[:, None, None] + term, state

    unused_state, states_out = lax.scan(backward, carried_total, tract_qd, reverse=True)
    state_in_b = states_in.astype(jnp.bfloat16).astype(jnp.float32)
    state_out_b = states_out.astype(jnp.bfloat16).astype(jnp.float32)
    in_weight = jnp.exp(-decay_rates[None, :] * (places + 1.0)[:, None])[None, :, :, None]
    out_weight = jnp.exp(-decay_rates[None, :] * (TRACT - places)[:, None])[None, :, :, None]
    pre_dq = grad_q + jnp.einsum("pthe,phde->pthd", pre_g.astype(jnp.float32), state_in_b) * in_weight
    pre_dk = grad_k + jnp.einsum("pthe,phde->pthd", pre_v.astype(jnp.float32), state_out_b) * out_weight
    pre_dv = grad_v + jnp.einsum("pthd,phde->pthe", pre_k.astype(jnp.float32), state_out_b) * out_weight
    flat = (PLEN, HEADS * D)
    resp_flat = (RESPONSES, RESP_LEN, HEADS * D)
    return (pre_dq.astype(jnp.bfloat16).reshape(flat), pre_dk.astype(jnp.bfloat16).reshape(flat), pre_dv.astype(jnp.bfloat16).reshape(flat), resp_dq.reshape(resp_flat), resp_dk.reshape(resp_flat), resp_dv.reshape(resp_flat))
```

```python
import functools

import jax
import jax.numpy as jnp
from jax import lax
from jax.experimental import pallas as pl
from jax.experimental.pallas import tpu as pltpu
from jax.sharding import PartitionSpec as P

D = 128
GROUP = 4
PAIR = 2
CHAIN = 32
RESPS = 16
PART = 16
F32 = jnp.float32
BF16 = jnp.bfloat16


def ring(step, size):
    return min(step % size, -step % size)


def exchange_places():
    places = {}
    for column in range(RESPS):
        x_to, yh_to, yl, z = column // 4, column % 4, column // 8, column % 8
        spots = [(l, k) for l in range(2) for k in range(8)]

        def hops(resp, spot):
            return (
                ring(resp // 4 - x_to, 4)
                + ring(2 * (resp % 4 - yh_to) + yl - spot[0], 8)
                + ring(spot[1] - z, 8)
            )

        for limit in range(16):
            taken = {}

            def assign(resp, seen):
                for spot in spots:
                    if hops(resp, spot) <= limit and spot not in seen:
                        seen.add(spot)
                        if spot not in taken or assign(taken[spot], seen):
                            taken[spot] = resp
                            return True
                return False

            if all(assign(resp, set()) for resp in range(RESPS)):
                break
        for (l, k), resp in taken.items():
            places[column, resp] = l * 8 + k
    return places


def exchange_pairs():
    pairs = []
    for (column, resp), chip in exchange_places().items():
        for core in range(2):
            pairs.append(((2 * column + core) * RESPS + resp, (2 * chip + core) * RESPS + column))
    return sorted(pairs)


def nt(a, b):
    return lax.dot_general(a, b, (((1,), (1,)), ((), ())), preferred_element_type=F32)


def tn(a, b):
    return lax.dot_general(a, b, (((0,), (0,)), ((), ())), preferred_element_type=F32)


def nn(a, b):
    return lax.dot_general(a, b, (((1,), (0,)), ((), ())), preferred_element_type=F32)


def rate_of(exps_ref, head, shape=(D, D)):
    return jnp.exp2(-jnp.full(shape, exps_ref[head].astype(F32), F32) / 1024.0)


def rows(shape=(D, D)):
    return lax.broadcasted_iota(jnp.int32, shape, 0).astype(F32)


def cut(head):
    return slice(head * D, (head + 1) * D)


def scaled(x, weight):
    return (x.astype(F32) * weight).astype(BF16)


def kv_kernel(exps, pk, pv, out):
    first = lax.axis_index("resp") * GROUP
    for h in range(GROUP):
        weight = jnp.exp(-rate_of(exps, first + h) * (D - 1.0 - rows()))
        kv = tn(scaled(pk[:, cut(h)], weight), pv[:, cut(h)]).astype(BF16)
        out[8 * h : 8 * h + 8] = kv.reshape(8, PART, D)


def masked_grad(rg, lengths, block, h):
    inside = lax.broadcasted_iota(jnp.int32, (D, D), 0) + block * D < lengths[0]
    grad = rg[0, cut(block), cut(h)]
    return jnp.where(inside, grad.astype(F32), 0.0).astype(BF16)


def qd_kernel(exps, lengths, pq, pg, rq, rg, qd_out, carried_out):
    first = lax.axis_index("resp") * GROUP
    for h in range(GROUP):
        weight = jnp.exp(-rate_of(exps, first + h) * rows())
        qd = tn(scaled(pq[:, cut(h)], weight), pg[:, cut(h)]).astype(BF16)
        qd_out[8 * h : 8 * h + 8] = qd.reshape(8, PART, D)
    first = lax.axis_index("prefix") * PAIR
    for h in range(PAIR):
        rate = rate_of(exps, first + h)
        carried = jnp.zeros((D, D), F32)
        for j in range(2):
            weight = jnp.exp(-rate * (rows() + float(j * D)))
            carried += tn(scaled(rq[0, cut(j), cut(h)], weight), masked_grad(rg, lengths, j, h))
        carried_out[8 * h : 8 * h + 8] = carried.astype(BF16).reshape(8, PART, D)


def decay_mask(rate):
    offsets = rows() - lax.broadcasted_iota(jnp.int32, (D, D), 1).astype(F32)
    return jnp.where(offsets >= 0.0, jnp.exp(-rate * jnp.maximum(offsets, 0.0)), 0.0)


def local_grads(q, k, v, g, mask):
    weights = (nt(q, k) * mask).astype(BF16)
    dscores = (nt(g, v) * mask).astype(BF16)
    return nn(dscores, k), tn(dscores, q), tn(weights, g)


def local_kernel(
    exps, lengths, pq, pk, pv, pg, rq, rk, rv, rg, pdq, pdk, pdv, rdq, rdk, rdv
):
    first = lax.axis_index("resp") * GROUP
    for h in range(GROUP):
        c = cut(h)
        mask = decay_mask(rate_of(exps, first + h))
        pdq[:, c], pdk[:, c], pdv[:, c] = local_grads(pq[:, c], pk[:, c], pv[:, c], pg[:, c], mask)
    first = lax.axis_index("prefix") * PAIR
    for h in range(PAIR):
        c = cut(h)
        rate = rate_of(exps, first + h)
        mask = decay_mask(rate)
        g0, g1 = (masked_grad(rg, lengths, j, h) for j in range(2))
        q0, q1 = rq[0, cut(0), c], rq[0, cut(1), c]
        k0, k1 = rk[0, cut(0), c], rk[0, cut(1), c]
        v0, v1 = rv[0, cut(0), c], rv[0, cut(1), c]
        resp_in = tn(scaled(k0, jnp.exp(-rate * (D - 1.0 - rows()))), v0).astype(BF16)
        resp_out = tn(scaled(q1, jnp.exp(-rate * rows())), g1).astype(BF16)
        dq, dk, dv = local_grads(q0, k0, v0, g0, mask)
        out_weight = jnp.exp(-rate * (float(D) - rows()))
        rdq[cut(0), c] = dq
        rdk[0, cut(0), c] = (dk + nt(v0, resp_out) * out_weight).astype(BF16)
        rdv[0, cut(0), c] = (dv + nn(k0, resp_out) * out_weight).astype(BF16)
        dq, dk, dv = local_grads(q1, k1, v1, g1, mask)
        rdq[cut(1), c] = dq + nt(g1, resp_in) * jnp.exp(-rate * (rows() + 1.0))
        rdk[0, cut(1), c] = dk.astype(BF16)
        rdv[0, cut(1), c] = dv.astype(BF16)


def tract_decay(exps):
    head = lax.axis_index("resp") * GROUP + lax.axis_index("prefix") // 8
    return jnp.exp(-rate_of(exps, head, (PART, D)) * float(D))


def forward_kernel(exps, kv, qd, carried, out):
    decay = tract_decay(exps)
    state = jnp.zeros((PART, D), F32)
    for b in range(CHAIN):
        out[b, 0:PART] = state.astype(BF16)
        state = state * decay + kv[b].astype(F32)
    start = state.astype(BF16)
    for b in range(CHAIN):
        out[b, PART : 2 * PART] = qd[b]
        out[b, 2 * PART : 3 * PART] = start
        out[b, 3 * PART : 4 * PART] = carried[b % 16]


def backward_kernel(exps, got, states, start):
    decay = tract_decay(exps)
    half = lax.axis_index("prefix") // 16
    state = jnp.zeros((PART, D), F32)
    for i in range(16):
        state = state + got[2 * i + half, 3 * PART : 4 * PART].astype(F32)
    for b in reversed(range(CHAIN)):
        states[b] = state.astype(BF16)
        state = state * decay + got[b, PART : 2 * PART].astype(F32)
    core = lax.axis_index("prefix") % 2
    for i in range(16):
        start[i] = got[16 * core + i, 2 * PART : 3 * PART]


def prefix_dq_kernel(exps, pg, got, pdq, out):
    first = lax.axis_index("resp") * GROUP
    for h in range(GROUP):
        c = cut(h)
        weight = jnp.exp(-rate_of(exps, first + h) * (rows() + 1.0))
        state_in = got[8 * h : 8 * h + 8, 0:PART].reshape(D, D)
        out[:, c] = (pdq[:, c] + nt(pg[:, c], state_in) * weight).astype(BF16)


def prefix_dkv_kernel(exps, pk, pv, states, pdk, pdv, dk, dv):
    first = lax.axis_index("resp") * GROUP
    for h in range(GROUP):
        c = cut(h)
        weight = jnp.exp(-rate_of(exps, first + h) * (float(D) - rows()))
        state_out = states[8 * h : 8 * h + 8].reshape(D, D)
        dk[:, c] = (pdk[:, c] + nt(pv[:, c], state_out) * weight).astype(BF16)
        dv[:, c] = (pdv[:, c] + nn(pk[:, c], state_out) * weight).astype(BF16)


def resp_dq_kernel(exps, lengths, rg, start, rdq, out):
    first = lax.axis_index("prefix") * PAIR
    for h in range(PAIR):
        c = cut(h)
        rate = rate_of(exps, first + h)
        state = start[8 * h : 8 * h + 8].reshape(D, D)
        for j in range(2):
            weight = jnp.exp(-rate * (rows() + float(j * D + 1)))
            term = nt(masked_grad(rg, lengths, j, h), state) * weight
            out[0, cut(j), c] = (rdq[cut(j), c] + term).astype(BF16)


def call(kernel, scalars, arrays, outs, flops):
    moved = sum(a.size * a.dtype.itemsize for a in arrays)
    moved += sum(o.size * o.dtype.itemsize for o in outs)
    return pl.pallas_call(
        kernel,
        out_shape=outs if len(outs) > 1 else outs[0],
        in_specs=[pl.BlockSpec(memory_space=pltpu.SMEM)] * len(scalars)
        + [pl.BlockSpec(memory_space=pltpu.VMEM)] * len(arrays),
        out_specs=[pl.BlockSpec(memory_space=pltpu.VMEM)] * len(outs)
        if len(outs) > 1
        else pl.BlockSpec(memory_space=pltpu.VMEM),
        cost_estimate=pl.CostEstimate(flops=flops, bytes_accessed=moved, transcendentals=0),
        name=kernel.__name__,
    )(*scalars, *arrays)


def shaped(shape, dtype):
    return jax.ShapeDtypeStruct(shape, dtype)


def local(there, back, pq, pk, pv, pg, rq, rk, rv, rg, lengths, exps):
    cube = 2 * D * D * D
    flat = (D, GROUP * D)
    slices = shaped((CHAIN, PART, D), BF16)
    pair = shaped((RESPS, PART, D), BF16)
    kv = call(kv_kernel, [exps], [pk, pv], [slices], 4 * cube)
    kv = lax.all_to_all(kv, "prefix", 0, 0)
    qd, carried = call(qd_kernel, [exps, lengths], [pq, pg, rq, rg], [slices, pair], 8 * cube)
    carried = lax.ppermute(carried, ("prefix", "resp"), there)
    resp_out = shaped(rq.shape, BF16)
    pdq, pdk, pdv, rdq, rdk, rdv = call(
        local_kernel,
        [exps, lengths],
        [pq, pk, pv, pg, rq, rk, rv, rg],
        [shaped(flat, F32)] * 3 + [shaped(rq.shape[1:], F32), resp_out, resp_out],
        48 * cube,
    )
    sent = call(
        forward_kernel, [exps], [kv, qd, carried], [shaped((CHAIN, 4 * PART, D), BF16)], cube
    )
    got = lax.all_to_all(sent, "prefix", 0, 0)
    states, start = call(backward_kernel, [exps], [got], [slices, pair], cube)
    states = lax.all_to_all(states, "prefix", 0, 0)
    start = lax.ppermute(start, ("prefix", "resp"), back)
    pre_dq = call(prefix_dq_kernel, [exps], [pg, got, pdq], [shaped(flat, BF16)], 4 * cube)
    resp_dq = call(resp_dq_kernel, [exps, lengths], [rg, start, rdq], [resp_out], 4 * cube)
    pre_dk, pre_dv = call(
        prefix_dkv_kernel, [exps], [pk, pv, states, pdk, pdv], [shaped(flat, BF16)] * 2, 8 * cube
    )
    return pre_dq, pre_dk, pre_dv, resp_dq, rdk, rdv


def solution(mesh):
    there = exchange_pairs()
    back = [(target, source) for source, target in there]
    prompt, response = P("prefix", "resp"), P("resp", None, "prefix")
    return jax.shard_map(
        functools.partial(local, there, back),
        mesh=mesh,
        in_specs=(prompt,) * 4 + (response,) * 4 + (P("resp"), P()),
        out_specs=(prompt,) * 3 + (response,) * 3,
        check_vma=False,
    )
```

```python
import functools

import jax
import jax.numpy as jnp
from jax import lax
from jax.experimental import pallas as pl
from jax.experimental.pallas import tpu as pltpu
from jax.sharding import PartitionSpec as P

D = 128
GROUP = 4
PAIR = 2
CHAIN = 32
RESPS = 16
PART = 16
F32 = jnp.float32
BF16 = jnp.bfloat16


def ring(source, target, size):
    step = (target - source) % size
    ways = []
    for sign, count in ((1, step), (-1, size - step)):
        if count <= size // 2:
            at, outside = source, 0
            for _ in range(count):
                to = (at + sign) % size
                outside += at // 4 != to // 4 or abs(at - to) > 1
                at = to
            ways.append(3 * count + 4 * outside)
    return sum(ways) / len(ways)


def exchange_places():
    places = {}
    spots = [(l, k) for l in range(2) for k in range(8)]
    for column in range(RESPS):
        yl, z = column // 8, column % 8

        def cost(resp, spot):
            return (
                ring(resp // 4, column // 4, 4)
                + ring(2 * (resp % 4) + yl, 2 * (column % 4) + spot[0], 8)
                + ring(z, spot[1], 8)
            )

        for limit in range(64):
            taken = {}

            def assign(resp, seen):
                for spot in spots:
                    if cost(resp, spot) <= limit and spot not in seen:
                        seen.add(spot)
                        if spot not in taken or assign(taken[spot], seen):
                            taken[spot] = resp
                            return True
                return False

            if all(assign(resp, set()) for resp in range(RESPS)):
                break
        for (l, k), resp in taken.items():
            places[column, resp] = l * 8 + k
    return places


def exchange_pairs():
    pairs = []
    for (column, resp), chip in exchange_places().items():
        for core in range(2):
            pairs.append(((2 * column + core) * RESPS + resp, (2 * chip + core) * RESPS + column))
    return sorted(pairs)


def nt(a, b):
    return lax.dot_general(a, b, (((1,), (1,)), ((), ())), preferred_element_type=F32)


def tn(a, b):
    return lax.dot_general(a, b, (((0,), (0,)), ((), ())), preferred_element_type=F32)


def nn(a, b):
    return lax.dot_general(a, b, (((1,), (0,)), ((), ())), preferred_element_type=F32)


def rate_of(exps_ref, head, shape=(D, D)):
    return jnp.exp2(-jnp.full(shape, exps_ref[head].astype(F32), F32) / 1024.0)


def rate_row(rates, index):
    return rates[8 * index : 8 * index + 1]


def rows(shape=(D, D)):
    return lax.broadcasted_iota(jnp.int32, shape, 0).astype(F32)


def cut(head):
    return slice(head * D, (head + 1) * D)


def scaled(x, weight):
    return (x.astype(F32) * weight).astype(BF16)


def owner(head, part):
    return 2 * (8 * (head % PAIR) + part) + head // PAIR


def parts_kernel(
    exps, lengths, pq_in, pk_in, pv_in, pg_in, rq_in, rg_in, out, carried_out, rates, masked,
    pq, pk, pv, pg, rq, rg, parts, loaded, stored,
):
    arrays = ((pk_in, pk), (pv_in, pv), (pq_in, pq), (pg_in, pg), (rq_in, rq), (rg_in, rg))
    loads = [pltpu.make_async_copy(a, b, loaded.at[i]) for i, (a, b) in enumerate(arrays)]
    for load in loads:
        load.start()
    mine, column = lax.axis_index("prefix"), lax.axis_index("resp")
    heads = [column * GROUP + h for h in range(GROUP)] + [mine * PAIR + h for h in range(PAIR)]
    for i, head in enumerate(heads):
        rates[8 * i : 8 * i + 8] = rate_of(exps, head, (8, D))
    tract = rate_of(exps, column * GROUP + mine % 2 * PAIR + mine // 16, (8, D))
    rates[48:56] = jnp.exp(-tract * float(D))
    stores = []
    for load in loads[:4]:
        load.wait()
    for h in range(GROUP):
        c = cut(h)
        rate = rate_row(rates, h)
        kv = tn(scaled(pk[:, c], jnp.exp(-rate * (D - 1.0 - rows()))), pv[:, c]).astype(BF16)
        qd = tn(scaled(pq[:, c], jnp.exp(-rate * rows())), pg[:, c]).astype(BF16)
        for k in range(8):
            parts[h, k, 0:PART] = kv[k * PART : (k + 1) * PART]
            parts[h, k, PART : 2 * PART] = qd[k * PART : (k + 1) * PART]
        store = pltpu.make_async_copy(
            parts.at[h], out.at[h % PAIR, :, h // PAIR], stored.at[h]
        )
        store.start()
        stores.append(store)
    for load in loads[4:]:
        load.wait()
    for h in range(PAIR):
        rate = rate_row(rates, GROUP + h)
        carried = jnp.zeros((D, D), F32)
        for j in range(2):
            inside = lax.broadcasted_iota(jnp.int32, (D, D), 0) + j * D < lengths[0]
            grad = jnp.where(inside, rg[0, cut(j), cut(h)].astype(F32), 0.0).astype(BF16)
            masked[cut(j), cut(h)] = grad
            weight = jnp.exp(-rate * (rows() + float(j * D)))
            carried += tn(scaled(rq[0, cut(j), cut(h)], weight), grad)
        carried_out[8 * h : 8 * h + 8] = carried.astype(BF16).reshape(8, PART, D)
    for store in stores:
        store.wait()


def decay_mask(rate):
    offsets = rows() - lax.broadcasted_iota(jnp.int32, (D, D), 1).astype(F32)
    return jnp.where(offsets >= 0.0, jnp.exp(-rate * jnp.maximum(offsets, 0.0)), 0.0)


def local_grads(q, k, v, g, mask):
    weights = (nt(q, k) * mask).astype(BF16)
    dscores = (nt(g, v) * mask).astype(BF16)
    return nn(dscores, k), tn(dscores, q), tn(weights, g)


def local_kernel(
    rates, pq, pk, pv, pg, rq, rk, rv, masked, after, pdq, pdk, pdv, rdq, rdk, rdv, token
):
    token[...] = jnp.zeros_like(token)
    for h in range(GROUP):
        c = cut(h)
        mask = decay_mask(rate_row(rates, h))
        pdq[:, c], pdk[:, c], pdv[:, c] = local_grads(pq[:, c], pk[:, c], pv[:, c], pg[:, c], mask)
    for h in range(PAIR):
        c = cut(h)
        rate = rate_row(rates, GROUP + h)
        mask = decay_mask(rate)
        g0, g1 = masked[cut(0), c], masked[cut(1), c]
        q0, q1 = rq[0, cut(0), c], rq[0, cut(1), c]
        k0, k1 = rk[0, cut(0), c], rk[0, cut(1), c]
        v0, v1 = rv[0, cut(0), c], rv[0, cut(1), c]
        resp_in = tn(scaled(k0, jnp.exp(-rate * (D - 1.0 - rows()))), v0).astype(BF16)
        resp_out = tn(scaled(q1, jnp.exp(-rate * rows())), g1).astype(BF16)
        dq, dk, dv = local_grads(q0, k0, v0, g0, mask)
        out_weight = jnp.exp(-rate * (float(D) - rows()))
        rdq[cut(0), c] = dq
        rdk[0, cut(0), c] = (dk + nt(v0, resp_out) * out_weight).astype(BF16)
        rdv[0, cut(0), c] = (dv + nn(k0, resp_out) * out_weight).astype(BF16)
        dq, dk, dv = local_grads(q1, k1, v1, g1, mask)
        rdq[cut(1), c] = dq + nt(g1, resp_in) * jnp.exp(-rate * (rows() + 1.0))
        rdk[0, cut(1), c] = dk.astype(BF16)
        rdv[0, cut(1), c] = dv.astype(BF16)


def start_kernel(rates, got, carried, out, token):
    decay = rates[48:49]
    state = jnp.zeros((PART, D), F32)
    for b in range(CHAIN):
        state = state * decay + got[b, 0:PART].astype(F32)
    start = state.astype(BF16)
    for j in range(RESPS):
        out[j, 0:PART] = start
        out[j, PART : 2 * PART] = carried[j]
    token[...] = jnp.zeros_like(token)


def states_kernel(rates, got, got_two, after, out, start):
    decay = rates[48:49]
    ahead = jnp.zeros((PART, D), F32)
    behind = jnp.zeros((PART, D), F32)
    for j in range(RESPS):
        behind = behind + got_two[j, PART : 2 * PART].astype(F32)
    for b in range(CHAIN):
        out[b, 0:PART] = ahead.astype(BF16)
        ahead = ahead * decay + got[b, 0:PART].astype(F32)
        e = CHAIN - 1 - b
        out[e, PART : 2 * PART] = behind.astype(BF16)
        behind = behind * decay + got[e, PART : 2 * PART].astype(F32)
    for j in range(RESPS):
        start[j] = got_two[j, 0:PART]


def prefix_kernel(rates, pk, pv, pg, states, pdq, pdk, pdv, dq, dk, dv):
    for h in range(GROUP):
        c = cut(h)
        rate = rate_row(rates, h)
        both = [states[owner(h, k)] for k in range(8)]
        state_in = jnp.concatenate([b[0:PART] for b in both], axis=0)
        state_out = jnp.concatenate([b[PART : 2 * PART] for b in both], axis=0)
        weight = jnp.exp(-rate * (rows() + 1.0))
        dq[:, c] = (pdq[:, c] + nt(pg[:, c], state_in) * weight).astype(BF16)
        weight = jnp.exp(-rate * (float(D) - rows()))
        dk[:, c] = (pdk[:, c] + nt(pv[:, c], state_out) * weight).astype(BF16)
        dv[:, c] = (pdv[:, c] + nn(pk[:, c], state_out) * weight).astype(BF16)


def resp_dq_kernel(rates, masked, start, rdq, out):
    for h in range(PAIR):
        c = cut(h)
        rate = rate_row(rates, GROUP + h)
        state = start[8 * h : 8 * h + 8].reshape(D, D)
        for j in range(2):
            weight = jnp.exp(-rate * (rows() + float(j * D + 1)))
            term = nt(masked[cut(j), c], state) * weight
            out[0, cut(j), c] = (rdq[cut(j), c] + term).astype(BF16)


def call(kernel, arrays, outs, flops, in_specs=None, out_specs=None, scratch_shapes=(), limit=8):
    moved = sum(a.size * a.dtype.itemsize for a in arrays)
    moved += sum(o.size * o.dtype.itemsize for o in outs)
    vmem = pl.BlockSpec(memory_space=pltpu.VMEM)
    got = pl.pallas_call(
        kernel,
        out_shape=tuple(outs),
        in_specs=in_specs or [vmem] * len(arrays),
        out_specs=tuple(out_specs or [vmem] * len(outs)),
        scratch_shapes=scratch_shapes,
        cost_estimate=pl.CostEstimate(flops=flops, bytes_accessed=moved, transcendentals=0),
        compiler_params=pltpu.CompilerParams(vmem_limit_bytes=limit << 20),
        name=kernel.__name__,
    )(*arrays)
    return got if len(outs) > 1 else got[0]


def shaped(shape, dtype):
    return jax.ShapeDtypeStruct(shape, dtype)


def local(there, back, pq, pk, pv, pg, rq, rk, rv, rg, lengths, exps):
    cube = 2 * D * D * D
    flat = (D, GROUP * D)
    token = shaped((8, D), F32)
    slots = shaped((CHAIN, 2 * PART, D), BF16)
    pair = shaped((RESPS, PART, D), BF16)
    resp_out = shaped(rq.shape, BF16)
    cores = [list(range(core, CHAIN, 2)) for core in range(2)]
    smem, hbm, vmem = (pl.BlockSpec(memory_space=m) for m in (pltpu.SMEM, pltpu.HBM, pltpu.VMEM))
    rates = shaped((56, D), F32)
    masked = shaped(rq.shape[1:], BF16)
    sources = [pq, pk, pv, pg, rq, rg]
    parts, carried, rates, masked = call(
        parts_kernel,
        [exps, lengths] + sources,
        [shaped((PAIR, 8, PAIR, 2 * PART, D), BF16), pair, rates, masked],
        12 * cube,
        [smem, smem] + [hbm] * 6,
        [hbm, vmem, vmem, vmem],
        [pltpu.VMEM(a.shape, a.dtype) for a in sources]
        + [pltpu.VMEM((GROUP, 8, 2 * PART, D), BF16)]
        + [pltpu.SemaphoreType.DMA((6,)), pltpu.SemaphoreType.DMA((GROUP,))],
        limit=60,
    )
    got = lax.all_to_all(parts.reshape(slots.shape), "prefix", 0, 0)
    carried = lax.ppermute(carried, ("prefix", "resp"), there)
    sent, after = call(
        start_kernel, [rates, got, carried], [shaped((RESPS, 2 * PART, D), BF16), token], cube
    )
    got_two = lax.all_to_all(sent, "prefix", 0, 0, axis_index_groups=cores)
    pdq, pdk, pdv, rdq, rdk, rdv, after = call(
        local_kernel,
        [rates, pq, pk, pv, pg, rq, rk, rv, masked, after],
        [shaped(flat, F32)] * 3 + [shaped(rq.shape[1:], F32), resp_out, resp_out, token],
        48 * cube,
    )
    states, start = call(states_kernel, [rates, got, got_two, after], [slots, pair], cube)
    states = lax.all_to_all(states, "prefix", 0, 0)
    start = lax.ppermute(start, ("prefix", "resp"), back)
    resp_dq = call(resp_dq_kernel, [rates, masked, start, rdq], [resp_out], 4 * cube)
    pre_dq, pre_dk, pre_dv = call(
        prefix_kernel,
        [rates, pk, pv, pg, states, pdq, pdk, pdv],
        [shaped(flat, BF16)] * 3,
        12 * cube,
    )
    return pre_dq, pre_dk, pre_dv, resp_dq, rdk, rdv


def solution(mesh):
    there = exchange_pairs()
    back = [(target, source) for source, target in there]
    prompt, response = P("prefix", "resp"), P("resp", None, "prefix")
    return jax.shard_map(
        functools.partial(local, there, back),
        mesh=mesh,
        in_specs=(prompt,) * 4 + (response,) * 4 + (P("resp"), P()),
        out_specs=(prompt,) * 3 + (response,) * 3,
        check_vma=False,
    )
```

```python
import functools

import jax
import jax.numpy as jnp
from jax import lax
from jax.experimental import pallas as pl
from jax.experimental.pallas import tpu as pltpu
from jax.sharding import PartitionSpec as P

D = 128
GROUP = 4
PAIR = 2
CHAIN = 32
RESPS = 16
PART = 16
F32 = jnp.float32
BF16 = jnp.bfloat16


GATHER = (
    "4c263da7fe805b91",
    "35df7eca248906b1",
    "846eb2fda350917c",
    "f9d7ea40cb268315",
    "1ab709d238e56fc4",
    "428e319b60ac57fd",
    "6429803ad7fbe51c",
    "c804962bae73df51",
    "ea08c9154b26df73",
    "7b9153806eca4df2",
    "20ca146987ed35fb",
    "b351826d940fca7e",
    "fd53be461ac78920",
    "0ac67fd528e419b3",
    "7fbd65ce412903a8",
    "e62af74d851c903b",
)
SPREAD = (
    "dcf54ea32b806791",
    "45df7ce2108936ba",
    "856eb0dfa243917c",
    "fd67e915cb348a20",
    "7fd298e10a463bc5",
    "28ae019763bc54fd",
    "7589c12ad43be60f",
    "ae51b923cd648f70",
    "8a01ef96cd743b25",
    "78914fb25de36ca0",
    "2ac9157b86ef304d",
    "a3bcd206e47f9158",
    "bfc3ed461a528970",
    "0be64cd528f719a3",
    "74bf659ed13c02a8",
    "d684f7e9c51ba032",
)


def exchange_pairs(table):
    pairs = []
    for column in range(RESPS):
        for resp in range(RESPS):
            chip = int(table[column][resp], 16)
            for core in range(2):
                response = (2 * column + core) * RESPS + resp
                pairs.append((response, (2 * chip + core) * RESPS + column))
    return sorted(pairs)


def nt(a, b):
    return lax.dot_general(a, b, (((1,), (1,)), ((), ())), preferred_element_type=F32)


def tn(a, b):
    return lax.dot_general(a, b, (((0,), (0,)), ((), ())), preferred_element_type=F32)


def nn(a, b):
    return lax.dot_general(a, b, (((1,), (0,)), ((), ())), preferred_element_type=F32)


def rate_of(exps_ref, head, shape=(D, D)):
    return jnp.exp2(-jnp.full(shape, exps_ref[head].astype(F32), F32) / 1024.0)


def rate_row(rates, index):
    return rates[8 * index : 8 * index + 1]


def rows(shape=(D, D)):
    return lax.broadcasted_iota(jnp.int32, shape, 0).astype(F32)


def cut(head):
    return slice(head * D, (head + 1) * D)


def scaled(x, weight):
    return (x.astype(F32) * weight).astype(BF16)


def owner(head, part):
    return 2 * (8 * (head % PAIR) + part) + head // PAIR


def parts_kernel(
    exps_in, lengths_in, pq_in, pk_in, pv_in, pg_in, rq_in, rg_in,
    out, carried_out, rates_out, masked_out,
    exps, lengths, pq, pk, pv, pg, rq, rg, parts, carried, rates, masked, loaded, stored,
):
    def copies(pairs, sems):
        return [pltpu.make_async_copy(a, b, sems.at[i]) for i, (a, b) in enumerate(pairs)]

    loads = copies(
        ((exps_in, exps), (lengths_in, lengths), (rq_in, rq), (rg_in, rg))
        + ((pk_in, pk), (pv_in, pv), (pq_in, pq), (pg_in, pg)),
        loaded,
    )
    stores = copies(
        ((rates, rates_out), (masked, masked_out), (carried, carried_out))
        + tuple((parts.at[h], out.at[h % PAIR, :, h // PAIR]) for h in range(GROUP)),
        stored,
    )
    for load in loads:
        load.start()
    mine, column = lax.axis_index("prefix"), lax.axis_index("resp")
    heads = [column * GROUP + h for h in range(GROUP)] + [mine * PAIR + h for h in range(PAIR)]
    loads[0].wait()
    for i, head in enumerate(heads):
        rates[8 * i : 8 * i + 8] = rate_of(exps, head, (8, D))
    tract = rate_of(exps, column * GROUP + mine % 2 * PAIR + mine // 16, (8, D))
    rates[48:56] = jnp.exp(-tract * float(D))
    stores[0].start()
    for load in loads[1:4]:
        load.wait()
    for h in range(PAIR):
        rate = rate_row(rates, GROUP + h)
        total = jnp.zeros((D, D), F32)
        for j in range(2):
            inside = lax.broadcasted_iota(jnp.int32, (D, D), 0) + j * D < lengths[0]
            grad = jnp.where(inside, rg[0, cut(j), cut(h)].astype(F32), 0.0).astype(BF16)
            masked[cut(j), cut(h)] = grad
            weight = jnp.exp(-rate * (rows() + float(j * D)))
            total += tn(scaled(rq[0, cut(j), cut(h)], weight), grad)
        carried[8 * h : 8 * h + 8] = total.astype(BF16).reshape(8, PART, D)
    stores[1].start()
    stores[2].start()
    for load in loads[4:]:
        load.wait()
    for h in range(GROUP):
        c = cut(h)
        rate = rate_row(rates, h)
        kv = tn(scaled(pk[:, c], jnp.exp(-rate * (D - 1.0 - rows()))), pv[:, c]).astype(BF16)
        qd = tn(scaled(pq[:, c], jnp.exp(-rate * rows())), pg[:, c]).astype(BF16)
        for k in range(8):
            parts[h, k, 0:PART] = kv[k * PART : (k + 1) * PART]
            parts[h, k, PART : 2 * PART] = qd[k * PART : (k + 1) * PART]
        stores[3 + h].start()
    for store in stores:
        store.wait()


def decay_mask(rate):
    offsets = rows() - lax.broadcasted_iota(jnp.int32, (D, D), 1).astype(F32)
    return jnp.where(offsets >= 0.0, jnp.exp(-rate * jnp.maximum(offsets, 0.0)), 0.0)


def local_grads(q, k, v, g, mask):
    weights = (nt(q, k) * mask).astype(BF16)
    dscores = (nt(g, v) * mask).astype(BF16)
    return nn(dscores, k), tn(dscores, q), tn(weights, g)


def local_kernel(
    rates, pq, pk, pv, pg, rq, rk, rv, masked, after, pdq, pdk, pdv, rdq, rdk, rdv, token
):
    token[...] = jnp.zeros_like(token)
    for h in range(GROUP):
        c = cut(h)
        mask = decay_mask(rate_row(rates, h))
        pdq[:, c], pdk[:, c], pdv[:, c] = local_grads(pq[:, c], pk[:, c], pv[:, c], pg[:, c], mask)
    for h in range(PAIR):
        c = cut(h)
        rate = rate_row(rates, GROUP + h)
        mask = decay_mask(rate)
        g0, g1 = masked[cut(0), c], masked[cut(1), c]
        q0, q1 = rq[0, cut(0), c], rq[0, cut(1), c]
        k0, k1 = rk[0, cut(0), c], rk[0, cut(1), c]
        v0, v1 = rv[0, cut(0), c], rv[0, cut(1), c]
        resp_in = tn(scaled(k0, jnp.exp(-rate * (D - 1.0 - rows()))), v0).astype(BF16)
        resp_out = tn(scaled(q1, jnp.exp(-rate * rows())), g1).astype(BF16)
        dq, dk, dv = local_grads(q0, k0, v0, g0, mask)
        out_weight = jnp.exp(-rate * (float(D) - rows()))
        rdq[cut(0), c] = dq
        rdk[0, cut(0), c] = (dk + nt(v0, resp_out) * out_weight).astype(BF16)
        rdv[0, cut(0), c] = (dv + nn(k0, resp_out) * out_weight).astype(BF16)
        dq, dk, dv = local_grads(q1, k1, v1, g1, mask)
        rdq[cut(1), c] = dq + nt(g1, resp_in) * jnp.exp(-rate * (rows() + 1.0))
        rdk[0, cut(1), c] = dk.astype(BF16)
        rdv[0, cut(1), c] = dv.astype(BF16)


def start_kernel(rates, got, carried, out, token):
    decay = rates[48:49]
    state = jnp.zeros((PART, D), F32)
    for b in range(CHAIN):
        state = state * decay + got[b, 0:PART].astype(F32)
    start = state.astype(BF16)
    for j in range(RESPS):
        out[j, 0:PART] = start
        out[j, PART : 2 * PART] = carried[j]
    token[...] = jnp.zeros_like(token)


def states_kernel(rates, got, got_two, after, out, start):
    decay = rates[48:49]
    ahead = jnp.zeros((PART, D), F32)
    behind = jnp.zeros((PART, D), F32)
    for j in range(RESPS):
        behind = behind + got_two[j, PART : 2 * PART].astype(F32)
    for b in range(CHAIN):
        out[b, 0:PART] = ahead.astype(BF16)
        ahead = ahead * decay + got[b, 0:PART].astype(F32)
        e = CHAIN - 1 - b
        out[e, PART : 2 * PART] = behind.astype(BF16)
        behind = behind * decay + got[e, PART : 2 * PART].astype(F32)
    for j in range(RESPS):
        start[j] = got_two[j, 0:PART]


def prefix_kernel(rates, pk, pv, pg, states, pdq, pdk, pdv, dq, dk, dv):
    for h in range(GROUP):
        c = cut(h)
        rate = rate_row(rates, h)
        both = [states[owner(h, k)] for k in range(8)]
        state_in = jnp.concatenate([b[0:PART] for b in both], axis=0)
        state_out = jnp.concatenate([b[PART : 2 * PART] for b in both], axis=0)
        weight = jnp.exp(-rate * (rows() + 1.0))
        dq[:, c] = (pdq[:, c] + nt(pg[:, c], state_in) * weight).astype(BF16)
        weight = jnp.exp(-rate * (float(D) - rows()))
        dk[:, c] = (pdk[:, c] + nt(pv[:, c], state_out) * weight).astype(BF16)
        dv[:, c] = (pdv[:, c] + nn(pk[:, c], state_out) * weight).astype(BF16)


def resp_dq_kernel(rates, masked, start, rdq, out):
    for h in range(PAIR):
        c = cut(h)
        rate = rate_row(rates, GROUP + h)
        state = start[8 * h : 8 * h + 8].reshape(D, D)
        for j in range(2):
            weight = jnp.exp(-rate * (rows() + float(j * D + 1)))
            term = nt(masked[cut(j), c], state) * weight
            out[0, cut(j), c] = (rdq[cut(j), c] + term).astype(BF16)


def call(kernel, arrays, outs, flops, in_specs=None, out_specs=None, scratch_shapes=(), limit=8 << 20):
    moved = sum(a.size * a.dtype.itemsize for a in arrays)
    moved += sum(o.size * o.dtype.itemsize for o in outs)
    vmem = pl.BlockSpec(memory_space=pltpu.VMEM)
    got = pl.pallas_call(
        kernel,
        out_shape=tuple(outs),
        in_specs=in_specs or [vmem] * len(arrays),
        out_specs=tuple(out_specs or [vmem] * len(outs)),
        scratch_shapes=scratch_shapes,
        cost_estimate=pl.CostEstimate(flops=flops, bytes_accessed=moved, transcendentals=0),
        compiler_params=pltpu.CompilerParams(vmem_limit_bytes=limit),
        name=kernel.__name__,
    )(*arrays)
    return got if len(outs) > 1 else got[0]


def shaped(shape, dtype):
    return jax.ShapeDtypeStruct(shape, dtype)


def local(there, back, pq, pk, pv, pg, rq, rk, rv, rg, lengths, exps):
    cube = 2 * D * D * D
    flat = (D, GROUP * D)
    token = shaped((8, D), F32)
    slots = shaped((CHAIN, 2 * PART, D), BF16)
    pair = shaped((RESPS, PART, D), BF16)
    resp_out = shaped(rq.shape, BF16)
    cores = [list(range(core, CHAIN, 2)) for core in range(2)]
    hbm = pl.BlockSpec(memory_space=pltpu.HBM)
    rates = shaped((56, D), F32)
    masked = shaped(rq.shape[1:], BF16)
    sources = [pq, pk, pv, pg, rq, rg]
    parts, carried, rates, masked = call(
        parts_kernel,
        [exps, lengths] + sources,
        [shaped((PAIR, 8, PAIR, 2 * PART, D), BF16), pair, rates, masked],
        12 * cube,
        [hbm] * 8,
        [hbm] * 4,
        [pltpu.SMEM(a.shape, a.dtype) for a in (exps, lengths)]
        + [pltpu.VMEM(a.shape, a.dtype) for a in sources]
        + [pltpu.VMEM((GROUP, 8, 2 * PART, D), BF16)]
        + [pltpu.VMEM(a.shape, a.dtype) for a in (pair, rates, masked)]
        + [pltpu.SemaphoreType.DMA((8,)), pltpu.SemaphoreType.DMA((3 + GROUP,))],
        limit=None,
    )
    got = lax.all_to_all(parts.reshape(slots.shape), "prefix", 0, 0)
    carried = lax.ppermute(carried, ("prefix", "resp"), there)
    sent, after = call(
        start_kernel, [rates, got, carried], [shaped((RESPS, 2 * PART, D), BF16), token], cube
    )
    got_two = lax.all_to_all(sent, "prefix", 0, 0, axis_index_groups=cores)
    pdq, pdk, pdv, rdq, rdk, rdv, after = call(
        local_kernel,
        [rates, pq, pk, pv, pg, rq, rk, rv, masked, after],
        [shaped(flat, F32)] * 3 + [shaped(rq.shape[1:], F32), resp_out, resp_out, token],
        48 * cube,
    )
    states, start = call(states_kernel, [rates, got, got_two, after], [slots, pair], cube)
    states = lax.all_to_all(states, "prefix", 0, 0)
    start = lax.ppermute(start, ("prefix", "resp"), back)
    resp_dq = call(resp_dq_kernel, [rates, masked, start, rdq], [resp_out], 4 * cube)
    pre_dq, pre_dk, pre_dv = call(
        prefix_kernel,
        [rates, pk, pv, pg, states, pdq, pdk, pdv],
        [shaped(flat, BF16)] * 3,
        12 * cube,
    )
    return pre_dq, pre_dk, pre_dv, resp_dq, rdk, rdv


def solution(mesh):
    there = exchange_pairs(GATHER)
    back = [(partner, response) for response, partner in exchange_pairs(SPREAD)]
    prompt, response = P("prefix", "resp"), P("resp", None, "prefix")
    return jax.shard_map(
        functools.partial(local, there, back),
        mesh=mesh,
        in_specs=(prompt,) * 4 + (response,) * 4 + (P("resp"), P()),
        out_specs=(prompt,) * 3 + (response,) * 3,
        check_vma=False,
    )
```

```python
import functools

import jax
import jax.numpy as jnp
from jax import lax
from jax.experimental import pallas as pl
from jax.experimental.pallas import tpu as pltpu
from jax.sharding import PartitionSpec as P

D = 128
GROUP = 4
PAIR = 2
CHAIN = 32
RESPS = 16
PART = 16
F32 = jnp.float32
BF16 = jnp.bfloat16


GATHER = (
    "5ca74d96ef013b82",
    "4dfa7ce836b90521",
    "906eb47fa18d235c",
    "ec4fda169b058327",
    "1ac789e60bd23f45",
    "71bf2935e0846acd",
    "d51ac023f79be648",
    "9d82ac135f4b7e60",
    "e813cf274b95da06",
    "6c9035a17df24eb8",
    "23fb15e9046ca7d8",
    "a250c378d14f9b6e",
    "fb5d2c478a6309e1",
    "3ae50bfd296c1847",
    "748c6e9f532d01ab",
    "f64ce758d02a913b",
)
SPREAD = (
    "4cf5dea26b803791",
    "4def75cb1089263a",
    "c06e895da243b17f",
    "fd67ec159b248a30",
    "29d608b1fa437ec5",
    "3b8e09af217c546d",
    "d528c09af43be617",
    "cd54b923ae618f70",
    "9802ef73cd64ba15",
    "6891fca25d374eb0",
    "2a4b38d9076f15ec",
    "b3a8c10de47f9256",
    "fd57bc43ae618920",
    "3ae4c8d509f612b7",
    "709e64fd51a8c32b",
    "d64ce7098f1ba532",
)


def exchange_pairs(table):
    pairs = []
    for column in range(RESPS):
        for resp in range(RESPS):
            chip = int(table[column][resp], 16)
            for core in range(2):
                response = (2 * column + core) * RESPS + resp
                pairs.append((response, (2 * chip + core) * RESPS + column))
    return sorted(pairs)


def nt(a, b):
    return lax.dot_general(a, b, (((1,), (1,)), ((), ())), preferred_element_type=F32)


def tn(a, b):
    return lax.dot_general(a, b, (((0,), (0,)), ((), ())), preferred_element_type=F32)


def nn(a, b):
    return lax.dot_general(a, b, (((1,), (0,)), ((), ())), preferred_element_type=F32)


def rate_of(exps_ref, head, shape=(D, D)):
    return jnp.exp2(-jnp.full(shape, exps_ref[head].astype(F32), F32) / 1024.0)


def rate_row(rates, index):
    return rates[8 * index : 8 * index + 1]


def rows(shape=(D, D)):
    return lax.broadcasted_iota(jnp.int32, shape, 0).astype(F32)


def cut(head):
    return slice(head * D, (head + 1) * D)


def scaled(x, weight):
    return (x.astype(F32) * weight).astype(BF16)


def owner(head, part):
    return 2 * (8 * (head % PAIR) + part) + head // PAIR


def parts_kernel(
    exps_in, pq_in, pk_in, pv_in, pg_in, out, rates_out,
    exps, pq, pk, pv, pg, parts, rates, loaded, stored,
):
    def copies(pairs, sems):
        return [pltpu.make_async_copy(a, b, sems.at[i]) for i, (a, b) in enumerate(pairs)]

    loads = copies(
        ((exps_in, exps), (pk_in, pk), (pv_in, pv), (pq_in, pq), (pg_in, pg)), loaded
    )
    stores = copies(
        ((rates, rates_out),)
        + tuple((parts.at[h], out.at[h % PAIR, :, h // PAIR]) for h in range(GROUP)),
        stored,
    )
    for load in loads:
        load.start()
    mine, column = lax.axis_index("prefix"), lax.axis_index("resp")
    heads = [column * GROUP + h for h in range(GROUP)] + [mine * PAIR + h for h in range(PAIR)]
    loads[0].wait()
    for i, head in enumerate(heads):
        rates[8 * i : 8 * i + 8] = rate_of(exps, head, (8, D))
    tract = rate_of(exps, column * GROUP + mine % 2 * PAIR + mine // 16, (8, D))
    rates[48:56] = jnp.exp(-tract * float(D))
    stores[0].start()
    for load in loads[1:]:
        load.wait()
    for h in range(GROUP):
        c = cut(h)
        rate = rate_row(rates, h)
        kv = tn(scaled(pk[:, c], jnp.exp(-rate * (D - 1.0 - rows()))), pv[:, c]).astype(BF16)
        qd = tn(scaled(pq[:, c], jnp.exp(-rate * rows())), pg[:, c]).astype(BF16)
        for k in range(8):
            parts[h, k, 0:PART] = kv[k * PART : (k + 1) * PART]
            parts[h, k, PART : 2 * PART] = qd[k * PART : (k + 1) * PART]
        stores[1 + h].start()
    for store in stores:
        store.wait()


def carried_kernel(lengths, rates, rq, rg, carried, masked):
    for h in range(PAIR):
        rate = rate_row(rates, GROUP + h)
        total = jnp.zeros((D, D), F32)
        for j in range(2):
            inside = lax.broadcasted_iota(jnp.int32, (D, D), 0) + j * D < lengths[0]
            grad = jnp.where(inside, rg[0, cut(j), cut(h)].astype(F32), 0.0).astype(BF16)
            masked[cut(j), cut(h)] = grad
            weight = jnp.exp(-rate * (rows() + float(j * D)))
            total += tn(scaled(rq[0, cut(j), cut(h)], weight), grad)
        carried[8 * h : 8 * h + 8] = total.astype(BF16).reshape(8, PART, D)


def decay_mask(rate):
    offsets = rows() - lax.broadcasted_iota(jnp.int32, (D, D), 1).astype(F32)
    return jnp.where(offsets >= 0.0, jnp.exp(-rate * jnp.maximum(offsets, 0.0)), 0.0)


def local_grads(q, k, v, g, mask):
    weights = (nt(q, k) * mask).astype(BF16)
    dscores = (nt(g, v) * mask).astype(BF16)
    return nn(dscores, k), tn(dscores, q), tn(weights, g)


def local_kernel(rates, pq, pk, pv, pg, pdq, pdk, pdv, token):
    token[...] = jnp.zeros_like(token)
    for h in range(GROUP):
        c = cut(h)
        mask = decay_mask(rate_row(rates, h))
        pdq[:, c], pdk[:, c], pdv[:, c] = local_grads(pq[:, c], pk[:, c], pv[:, c], pg[:, c], mask)


def resp_kernel(rates, rq, rk, rv, masked, after, rdq, rdk, rdv):
    for h in range(PAIR):
        c = cut(h)
        rate = rate_row(rates, GROUP + h)
        mask = decay_mask(rate)
        g0, g1 = masked[cut(0), c], masked[cut(1), c]
        q0, q1 = rq[0, cut(0), c], rq[0, cut(1), c]
        k0, k1 = rk[0, cut(0), c], rk[0, cut(1), c]
        v0, v1 = rv[0, cut(0), c], rv[0, cut(1), c]
        resp_in = tn(scaled(k0, jnp.exp(-rate * (D - 1.0 - rows()))), v0).astype(BF16)
        resp_out = tn(scaled(q1, jnp.exp(-rate * rows())), g1).astype(BF16)
        dq, dk, dv = local_grads(q0, k0, v0, g0, mask)
        out_weight = jnp.exp(-rate * (float(D) - rows()))
        rdq[cut(0), c] = dq
        rdk[0, cut(0), c] = (dk + nt(v0, resp_out) * out_weight).astype(BF16)
        rdv[0, cut(0), c] = (dv + nn(k0, resp_out) * out_weight).astype(BF16)
        dq, dk, dv = local_grads(q1, k1, v1, g1, mask)
        rdq[cut(1), c] = dq + nt(g1, resp_in) * jnp.exp(-rate * (rows() + 1.0))
        rdk[0, cut(1), c] = dk.astype(BF16)
        rdv[0, cut(1), c] = dv.astype(BF16)


def start_kernel(rates, got, carried, before, out):
    decay = rates[48:49]
    state = jnp.zeros((PART, D), F32)
    for b in range(CHAIN):
        state = state * decay + got[b, 0:PART].astype(F32)
    start = state.astype(BF16)
    for j in range(RESPS):
        out[j, 0:PART] = start
        out[j, PART : 2 * PART] = carried[j]


def states_kernel(rates, got, got_two, out, start, token):
    decay = rates[48:49]
    ahead = jnp.zeros((PART, D), F32)
    behind = jnp.zeros((PART, D), F32)
    for j in range(RESPS):
        behind = behind + got_two[j, PART : 2 * PART].astype(F32)
    for b in range(CHAIN):
        out[b, 0:PART] = ahead.astype(BF16)
        ahead = ahead * decay + got[b, 0:PART].astype(F32)
        e = CHAIN - 1 - b
        out[e, PART : 2 * PART] = behind.astype(BF16)
        behind = behind * decay + got[e, PART : 2 * PART].astype(F32)
    for j in range(RESPS):
        start[j] = got_two[j, 0:PART]
    token[...] = jnp.zeros_like(token)


def final_kernel(
    rates, pk, pv, pg, states, pdq, pdk, pdv, masked, start, rdq, dq, dk, dv, resp_dq
):
    for h in range(PAIR):
        c = cut(h)
        rate = rate_row(rates, GROUP + h)
        state = start[8 * h : 8 * h + 8].reshape(D, D)
        for j in range(2):
            weight = jnp.exp(-rate * (rows() + float(j * D + 1)))
            term = nt(masked[cut(j), c], state) * weight
            resp_dq[0, cut(j), c] = (rdq[cut(j), c] + term).astype(BF16)
    for h in range(GROUP):
        c = cut(h)
        rate = rate_row(rates, h)
        both = [states[owner(h, k)] for k in range(8)]
        state_in = jnp.concatenate([b[0:PART] for b in both], axis=0)
        state_out = jnp.concatenate([b[PART : 2 * PART] for b in both], axis=0)
        weight = jnp.exp(-rate * (rows() + 1.0))
        dq[:, c] = (pdq[:, c] + nt(pg[:, c], state_in) * weight).astype(BF16)
        weight = jnp.exp(-rate * (float(D) - rows()))
        dk[:, c] = (pdk[:, c] + nt(pv[:, c], state_out) * weight).astype(BF16)
        dv[:, c] = (pdv[:, c] + nn(pk[:, c], state_out) * weight).astype(BF16)


def call(kernel, arrays, outs, flops, in_specs=None, out_specs=None, scratch_shapes=(), limit=8 << 20):
    moved = sum(a.size * a.dtype.itemsize for a in arrays)
    moved += sum(o.size * o.dtype.itemsize for o in outs)
    vmem = pl.BlockSpec(memory_space=pltpu.VMEM)
    got = pl.pallas_call(
        kernel,
        out_shape=tuple(outs),
        in_specs=in_specs or [vmem] * len(arrays),
        out_specs=tuple(out_specs or [vmem] * len(outs)),
        scratch_shapes=scratch_shapes,
        cost_estimate=pl.CostEstimate(flops=flops, bytes_accessed=moved, transcendentals=0),
        compiler_params=pltpu.CompilerParams(vmem_limit_bytes=limit),
        name=kernel.__name__,
    )(*arrays)
    return got if len(outs) > 1 else got[0]


def shaped(shape, dtype):
    return jax.ShapeDtypeStruct(shape, dtype)


def local(there, back, pq, pk, pv, pg, rq, rk, rv, rg, lengths, exps):
    cube = 2 * D * D * D
    flat = (D, GROUP * D)
    token = shaped((8, D), F32)
    slots = shaped((CHAIN, 2 * PART, D), BF16)
    pair = shaped((RESPS, PART, D), BF16)
    resp_out = shaped(rq.shape, BF16)
    cores = [list(range(core, CHAIN, 2)) for core in range(2)]
    hbm = pl.BlockSpec(memory_space=pltpu.HBM)
    rates = shaped((56, D), F32)
    masked = shaped(rq.shape[1:], BF16)
    sources = [pq, pk, pv, pg]
    parts, rates = call(
        parts_kernel,
        [exps] + sources,
        [shaped((PAIR, 8, PAIR, 2 * PART, D), BF16), rates],
        8 * cube,
        [hbm] * 5,
        [hbm] * 2,
        [pltpu.SMEM(exps.shape, exps.dtype)]
        + [pltpu.VMEM(a.shape, a.dtype) for a in sources]
        + [pltpu.VMEM((GROUP, 8, 2 * PART, D), BF16), pltpu.VMEM(rates.shape, F32)]
        + [pltpu.SemaphoreType.DMA((5,)), pltpu.SemaphoreType.DMA((1 + GROUP,))],
        limit=None,
    )
    carried, masked = call(
        carried_kernel,
        [lengths, rates, rq, rg],
        [pair, masked],
        4 * cube,
        [pl.BlockSpec(memory_space=pltpu.SMEM)] + [pl.BlockSpec(memory_space=pltpu.VMEM)] * 3,
    )
    got = lax.all_to_all(parts.reshape(slots.shape), "prefix", 0, 0)
    carried = lax.ppermute(carried, ("prefix", "resp"), there)
    pdq, pdk, pdv, before = call(
        local_kernel, [rates, pq, pk, pv, pg], [shaped(flat, F32)] * 3 + [token], 20 * cube
    )
    sent = call(
        start_kernel, [rates, got, carried, before], [shaped((RESPS, 2 * PART, D), BF16)], cube
    )
    got_two = lax.all_to_all(sent, "prefix", 0, 0, axis_index_groups=cores)
    states, start, after = call(
        states_kernel, [rates, got, got_two], [slots, pair, token], cube
    )
    rdq, rdk, rdv = call(
        resp_kernel,
        [rates, rq, rk, rv, masked, after],
        [shaped(rq.shape[1:], F32), resp_out, resp_out],
        28 * cube,
    )
    states = lax.all_to_all(states, "prefix", 0, 0)
    start = lax.ppermute(start, ("prefix", "resp"), back)
    pre_dq, pre_dk, pre_dv, resp_dq = call(
        final_kernel,
        [rates, pk, pv, pg, states, pdq, pdk, pdv, masked, start, rdq],
        [shaped(flat, BF16)] * 3 + [resp_out],
        16 * cube,
    )
    return pre_dq, pre_dk, pre_dv, resp_dq, rdk, rdv


def solution(mesh):
    there = exchange_pairs(GATHER)
    back = [(partner, response) for response, partner in exchange_pairs(SPREAD)]
    prompt, response = P("prefix", "resp"), P("resp", None, "prefix")
    return jax.shard_map(
        functools.partial(local, there, back),
        mesh=mesh,
        in_specs=(prompt,) * 4 + (response,) * 4 + (P("resp"), P()),
        out_specs=(prompt,) * 3 + (response,) * 3,
        check_vma=False,
    )
```

```python
import functools

import jax
import jax.numpy as jnp
from jax import lax
from jax.experimental import pallas as pl
from jax.experimental.pallas import tpu as pltpu
from jax.sharding import PartitionSpec as P

D = 128
GROUP = 4
PAIR = 2
CHAIN = 32
RESPS = 16
PART = 16
F32 = jnp.float32
BF16 = jnp.bfloat16


GATHER = (
    "5ca74d96ef013b82",
    "4dfa7ce836b90521",
    "906eb47fa18d235c",
    "ec4fda169b058327",
    "1ac789e60bd23f45",
    "71bf2935e0846acd",
    "d51ac023f79be648",
    "9d82ac135f4b7e60",
    "e813cf274b95da06",
    "6c9035a17df24eb8",
    "23fb15e9046ca7d8",
    "a250c378d14f9b6e",
    "fb5d2c478a6309e1",
    "3ae50bfd296c1847",
    "748c6e9f532d01ab",
    "f64ce758d02a913b",
)
SPREAD = (
    "nvf7hpa2go806e91",
    "goefhpq82b193i0a",
    "80hrb1jpa2iq934c",
    "qd5h43j69b2ica1r",
    "2td5jrb3lae6ksc4",
    "7mfckuabltse645d",
    "f4nuc0tvd7l8e6m5",
    "9dnva81gue0m7f65",
    "oa01ge86hp75df29",
    "hp917oa2igf3bq80",
    "2a9b1jc80hip34rq",
    "b3jra29ed4isc15q",
    "9bcdse45la6krt32",
    "luc64td5fse7mkb3",
    "5fmc6e8d70tu4lnv",
    "e6duf7nv851a90mo",
)


def exchange_pairs(table, turn):
    pairs = []
    for column in range(RESPS):
        for resp in range(RESPS):
            at, chip = divmod(int(table[column][resp], 32), 16)
            if at == turn:
                for core in range(2):
                    response = (2 * column + core) * RESPS + resp
                    pairs.append((response, (2 * chip + core) * RESPS + column))
    return sorted(pairs)


def nt(a, b):
    return lax.dot_general(a, b, (((1,), (1,)), ((), ())), preferred_element_type=F32)


def tn(a, b):
    return lax.dot_general(a, b, (((0,), (0,)), ((), ())), preferred_element_type=F32)


def nn(a, b):
    return lax.dot_general(a, b, (((1,), (0,)), ((), ())), preferred_element_type=F32)


def rate_of(exps_ref, head, shape=(D, D)):
    return jnp.exp2(-jnp.full(shape, exps_ref[head].astype(F32), F32) / 1024.0)


def rate_row(rates, index):
    return rates[8 * index : 8 * index + 1]


def rows(shape=(D, D)):
    return lax.broadcasted_iota(jnp.int32, shape, 0).astype(F32)


def cut(head):
    return slice(head * D, (head + 1) * D)


def scaled(x, weight):
    return (x.astype(F32) * weight).astype(BF16)


def owner(head, part):
    return 2 * (8 * (head % PAIR) + part) + head // PAIR


def parts_kernel(
    exps_in, pq_in, pk_in, pv_in, pg_in, out, rates_out,
    exps, pq, pk, pv, pg, parts, rates, loaded, stored,
):
    def copies(pairs, sems):
        return [pltpu.make_async_copy(a, b, sems.at[i]) for i, (a, b) in enumerate(pairs)]

    loads = copies(
        ((exps_in, exps), (pk_in, pk), (pv_in, pv), (pq_in, pq), (pg_in, pg)), loaded
    )
    stores = copies(
        ((rates, rates_out),)
        + tuple((parts.at[h], out.at[h % PAIR, :, h // PAIR]) for h in range(GROUP)),
        stored,
    )
    for load in loads:
        load.start()
    mine, column = lax.axis_index("prefix"), lax.axis_index("resp")
    heads = [column * GROUP + h for h in range(GROUP)] + [mine * PAIR + h for h in range(PAIR)]
    loads[0].wait()
    for i, head in enumerate(heads):
        rates[8 * i : 8 * i + 8] = rate_of(exps, head, (8, D))
    tract = rate_of(exps, column * GROUP + mine % 2 * PAIR + mine // 16, (8, D))
    rates[48:56] = jnp.exp(-tract * float(D))
    stores[0].start()
    for load in loads[1:]:
        load.wait()
    for h in range(GROUP):
        c = cut(h)
        rate = rate_row(rates, h)
        kv = tn(scaled(pk[:, c], jnp.exp(-rate * (D - 1.0 - rows()))), pv[:, c]).astype(BF16)
        qd = tn(scaled(pq[:, c], jnp.exp(-rate * rows())), pg[:, c]).astype(BF16)
        for k in range(8):
            parts[h, k, 0:PART] = kv[k * PART : (k + 1) * PART]
            parts[h, k, PART : 2 * PART] = qd[k * PART : (k + 1) * PART]
        stores[1 + h].start()
    for store in stores:
        store.wait()


def carried_kernel(lengths, rates, rq, rg, carried, masked):
    for h in range(PAIR):
        rate = rate_row(rates, GROUP + h)
        total = jnp.zeros((D, D), F32)
        for j in range(2):
            inside = lax.broadcasted_iota(jnp.int32, (D, D), 0) + j * D < lengths[0]
            grad = jnp.where(inside, rg[0, cut(j), cut(h)].astype(F32), 0.0).astype(BF16)
            masked[cut(j), cut(h)] = grad
            weight = jnp.exp(-rate * (rows() + float(j * D)))
            total += tn(scaled(rq[0, cut(j), cut(h)], weight), grad)
        carried[8 * h : 8 * h + 8] = total.astype(BF16).reshape(8, PART, D)


def decay_mask(rate):
    offsets = rows() - lax.broadcasted_iota(jnp.int32, (D, D), 1).astype(F32)
    return jnp.where(offsets >= 0.0, jnp.exp(-rate * jnp.maximum(offsets, 0.0)), 0.0)


def local_grads(q, k, v, g, mask):
    weights = (nt(q, k) * mask).astype(BF16)
    dscores = (nt(g, v) * mask).astype(BF16)
    return nn(dscores, k), tn(dscores, q), tn(weights, g)


def local_kernel(rates, pq, pk, pv, pg, pdq, pdk, pdv, token):
    token[...] = jnp.zeros_like(token)
    for h in range(GROUP):
        c = cut(h)
        mask = decay_mask(rate_row(rates, h))
        pdq[:, c], pdk[:, c], pdv[:, c] = local_grads(pq[:, c], pk[:, c], pv[:, c], pg[:, c], mask)


def resp_kernel(rates, rq, rk, rv, masked, after, rdq, rdk, rdv):
    for h in range(PAIR):
        c = cut(h)
        rate = rate_row(rates, GROUP + h)
        mask = decay_mask(rate)
        g0, g1 = masked[cut(0), c], masked[cut(1), c]
        q0, q1 = rq[0, cut(0), c], rq[0, cut(1), c]
        k0, k1 = rk[0, cut(0), c], rk[0, cut(1), c]
        v0, v1 = rv[0, cut(0), c], rv[0, cut(1), c]
        resp_in = tn(scaled(k0, jnp.exp(-rate * (D - 1.0 - rows()))), v0).astype(BF16)
        resp_out = tn(scaled(q1, jnp.exp(-rate * rows())), g1).astype(BF16)
        dq, dk, dv = local_grads(q0, k0, v0, g0, mask)
        out_weight = jnp.exp(-rate * (float(D) - rows()))
        rdq[cut(0), c] = dq
        rdk[0, cut(0), c] = (dk + nt(v0, resp_out) * out_weight).astype(BF16)
        rdv[0, cut(0), c] = (dv + nn(k0, resp_out) * out_weight).astype(BF16)
        dq, dk, dv = local_grads(q1, k1, v1, g1, mask)
        rdq[cut(1), c] = dq + nt(g1, resp_in) * jnp.exp(-rate * (rows() + 1.0))
        rdk[0, cut(1), c] = dk.astype(BF16)
        rdv[0, cut(1), c] = dv.astype(BF16)


def start_kernel(rates, got, carried, before, out):
    decay = rates[48:49]
    state = jnp.zeros((PART, D), F32)
    for b in range(CHAIN):
        state = state * decay + got[b, 0:PART].astype(F32)
    start = state.astype(BF16)
    for j in range(RESPS):
        out[j, 0:PART] = start
        out[j, PART : 2 * PART] = carried[j]


def states_kernel(rates, got, got_two, out, start, token):
    decay = rates[48:49]
    ahead = jnp.zeros((PART, D), F32)
    behind = jnp.zeros((PART, D), F32)
    for j in range(RESPS):
        behind = behind + got_two[j, PART : 2 * PART].astype(F32)
    for b in range(CHAIN):
        out[b, 0:PART] = ahead.astype(BF16)
        ahead = ahead * decay + got[b, 0:PART].astype(F32)
        e = CHAIN - 1 - b
        out[e, PART : 2 * PART] = behind.astype(BF16)
        behind = behind * decay + got[e, PART : 2 * PART].astype(F32)
    for j in range(RESPS):
        start[j] = got_two[j, 0:PART]
    token[...] = jnp.zeros_like(token)


def final_kernel(
    rates, pk, pv, pg, states, pdq, pdk, pdv, masked, start, start_two, rdq, dq, dk, dv, resp_dq
):
    for h in range(PAIR):
        c = cut(h)
        rate = rate_row(rates, GROUP + h)
        cuts = slice(8 * h, 8 * h + 8)
        state = (start[cuts] + start_two[cuts]).reshape(D, D)
        for j in range(2):
            weight = jnp.exp(-rate * (rows() + float(j * D + 1)))
            term = nt(masked[cut(j), c], state) * weight
            resp_dq[0, cut(j), c] = (rdq[cut(j), c] + term).astype(BF16)
    for h in range(GROUP):
        c = cut(h)
        rate = rate_row(rates, h)
        both = [states[owner(h, k)] for k in range(8)]
        state_in = jnp.concatenate([b[0:PART] for b in both], axis=0)
        state_out = jnp.concatenate([b[PART : 2 * PART] for b in both], axis=0)
        weight = jnp.exp(-rate * (rows() + 1.0))
        dq[:, c] = (pdq[:, c] + nt(pg[:, c], state_in) * weight).astype(BF16)
        weight = jnp.exp(-rate * (float(D) - rows()))
        dk[:, c] = (pdk[:, c] + nt(pv[:, c], state_out) * weight).astype(BF16)
        dv[:, c] = (pdv[:, c] + nn(pk[:, c], state_out) * weight).astype(BF16)


def call(kernel, arrays, outs, flops, in_specs=None, out_specs=None, scratch_shapes=(), limit=8 << 20):
    moved = sum(a.size * a.dtype.itemsize for a in arrays)
    moved += sum(o.size * o.dtype.itemsize for o in outs)
    vmem = pl.BlockSpec(memory_space=pltpu.VMEM)
    got = pl.pallas_call(
        kernel,
        out_shape=tuple(outs),
        in_specs=in_specs or [vmem] * len(arrays),
        out_specs=tuple(out_specs or [vmem] * len(outs)),
        scratch_shapes=scratch_shapes,
        cost_estimate=pl.CostEstimate(flops=flops, bytes_accessed=moved, transcendentals=0),
        compiler_params=pltpu.CompilerParams(vmem_limit_bytes=limit),
        name=kernel.__name__,
    )(*arrays)
    return got if len(outs) > 1 else got[0]


def shaped(shape, dtype):
    return jax.ShapeDtypeStruct(shape, dtype)


def local(there, back, pq, pk, pv, pg, rq, rk, rv, rg, lengths, exps):
    cube = 2 * D * D * D
    flat = (D, GROUP * D)
    token = shaped((8, D), F32)
    slots = shaped((CHAIN, 2 * PART, D), BF16)
    pair = shaped((RESPS, PART, D), BF16)
    resp_out = shaped(rq.shape, BF16)
    cores = [list(range(core, CHAIN, 2)) for core in range(2)]
    hbm = pl.BlockSpec(memory_space=pltpu.HBM)
    rates = shaped((56, D), F32)
    masked = shaped(rq.shape[1:], BF16)
    sources = [pq, pk, pv, pg]
    parts, rates = call(
        parts_kernel,
        [exps] + sources,
        [shaped((PAIR, 8, PAIR, 2 * PART, D), BF16), rates],
        8 * cube,
        [hbm] * 5,
        [hbm] * 2,
        [pltpu.SMEM(exps.shape, exps.dtype)]
        + [pltpu.VMEM(a.shape, a.dtype) for a in sources]
        + [pltpu.VMEM((GROUP, 8, 2 * PART, D), BF16), pltpu.VMEM(rates.shape, F32)]
        + [pltpu.SemaphoreType.DMA((5,)), pltpu.SemaphoreType.DMA((1 + GROUP,))],
        limit=None,
    )
    carried, masked = call(
        carried_kernel,
        [lengths, rates, rq, rg],
        [pair, masked],
        4 * cube,
        [pl.BlockSpec(memory_space=pltpu.SMEM)] + [pl.BlockSpec(memory_space=pltpu.VMEM)] * 3,
    )
    got = lax.all_to_all(parts.reshape(slots.shape), "prefix", 0, 0)
    carried = lax.ppermute(carried, ("prefix", "resp"), there)
    pdq, pdk, pdv, before = call(
        local_kernel, [rates, pq, pk, pv, pg], [shaped(flat, F32)] * 3 + [token], 20 * cube
    )
    sent = call(
        start_kernel, [rates, got, carried, before], [shaped((RESPS, 2 * PART, D), BF16)], cube
    )
    got_two = lax.all_to_all(sent, "prefix", 0, 0, axis_index_groups=cores)
    states, start, after = call(
        states_kernel, [rates, got, got_two], [slots, pair, token], cube
    )
    rdq, rdk, rdv = call(
        resp_kernel,
        [rates, rq, rk, rv, masked, after],
        [shaped(rq.shape[1:], F32), resp_out, resp_out],
        28 * cube,
    )
    states = lax.all_to_all(states, "prefix", 0, 0)
    starts = [lax.ppermute(start, ("prefix", "resp"), pairs) for pairs in back]
    pre_dq, pre_dk, pre_dv, resp_dq = call(
        final_kernel,
        [rates, pk, pv, pg, states, pdq, pdk, pdv, masked, *starts, rdq],
        [shaped(flat, BF16)] * 3 + [resp_out],
        16 * cube,
    )
    return pre_dq, pre_dk, pre_dv, resp_dq, rdk, rdv


def solution(mesh):
    there = exchange_pairs(GATHER, 0)
    back = [[(b, a) for a, b in exchange_pairs(SPREAD, turn)] for turn in range(2)]
    prompt, response = P("prefix", "resp"), P("resp", None, "prefix")
    return jax.shard_map(
        functools.partial(local, there, back),
        mesh=mesh,
        in_specs=(prompt,) * 4 + (response,) * 4 + (P("resp"), P()),
        out_specs=(prompt,) * 3 + (response,) * 3,
        check_vma=False,
    )
```

```python
import functools

import jax
import jax.numpy as jnp
from jax import lax
from jax.experimental import pallas as pl
from jax.experimental.pallas import tpu as pltpu
from jax.sharding import PartitionSpec as P

D = 128
GROUP = 4
PAIR = 2
CHAIN = 32
RESPS = 16
PART = 16
F32 = jnp.float32
BF16 = jnp.bfloat16


GATHER = (
    "5ca74d96ef013b82",
    "4dfa7ce836b90521",
    "906eb47fa18d235c",
    "ec4fda169b058327",
    "1ac789e60bd23f45",
    "71bf2935e0846acd",
    "d51ac023f79be648",
    "9d82ac135f4b7e60",
    "e813cf274b95da06",
    "6c9035a17df24eb8",
    "23fb15e9046ca7d8",
    "a250c378d14f9b6e",
    "fb5d2c478a6309e1",
    "3ae50bfd296c1847",
    "748c6e9f532d01ab",
    "f64ce758d02a913b",
)
SPREAD = (
    "nvf7hpa2go806e91",
    "goefhpq82b193i0a",
    "80hrb1jpa2iq934c",
    "qd5h43j69b2ica1r",
    "2td5jrb3lae6ksc4",
    "7mfckuabltse645d",
    "f4nuc0tvd7l8e6m5",
    "9dnva81gue0m7f65",
    "oa01ge86hp75df29",
    "hp917oa2igf3bq80",
    "2a9b1jc80hip34rq",
    "b3jra29ed4isc15q",
    "9bcdse45la6krt32",
    "luc64td5fse7mkb3",
    "5fmc6e8d70tu4lnv",
    "e6duf7nv851a90mo",
)


def exchange_pairs(table, turn):
    pairs = []
    for column in range(RESPS):
        for resp in range(RESPS):
            at, chip = divmod(int(table[column][resp], 32), 16)
            if at == turn:
                for core in range(2):
                    response = (2 * column + core) * RESPS + resp
                    pairs.append((response, (2 * chip + core) * RESPS + column))
    return sorted(pairs)


def nt(a, b):
    return lax.dot_general(a, b, (((1,), (1,)), ((), ())), preferred_element_type=F32)


def tn(a, b):
    return lax.dot_general(a, b, (((0,), (0,)), ((), ())), preferred_element_type=F32)


def nn(a, b):
    return lax.dot_general(a, b, (((1,), (0,)), ((), ())), preferred_element_type=F32)


def rate_of(exps_ref, head, shape=(D, D)):
    return jnp.exp2(-jnp.full(shape, exps_ref[head].astype(F32), F32) / 1024.0)


def rate_row(rates, index):
    return rates[8 * index : 8 * index + 1]


def rows(shape=(D, D)):
    return lax.broadcasted_iota(jnp.int32, shape, 0).astype(F32)


def cut(head):
    return slice(head * D, (head + 1) * D)


def scaled(x, weight):
    return (x.astype(F32) * weight).astype(BF16)


def owner(head, part):
    return 2 * (8 * (head % PAIR) + part) + head // PAIR


def parts_kernel(
    exps_in, pq_in, pk_in, pv_in, pg_in, out, rates_out,
    exps, pq, pk, pv, pg, parts, rates, loaded, stored,
):
    def copies(pairs, sems):
        return [pltpu.make_async_copy(a, b, sems.at[i]) for i, (a, b) in enumerate(pairs)]

    loads = copies(
        ((exps_in, exps), (pk_in, pk), (pv_in, pv), (pq_in, pq), (pg_in, pg)), loaded
    )
    stores = copies(
        ((rates, rates_out),)
        + tuple((parts.at[h], out.at[h % PAIR, :, h // PAIR]) for h in range(GROUP)),
        stored,
    )
    for load in loads:
        load.start()
    mine, column = lax.axis_index("prefix"), lax.axis_index("resp")
    heads = [column * GROUP + h for h in range(GROUP)] + [mine * PAIR + h for h in range(PAIR)]
    loads[0].wait()
    for i, head in enumerate(heads):
        rates[8 * i : 8 * i + 8] = rate_of(exps, head, (8, D))
    tract = rate_of(exps, column * GROUP + mine % 2 * PAIR + mine // 16, (8, D))
    rates[48:56] = jnp.exp(-tract * float(D))
    stores[0].start()
    for load in loads[1:]:
        load.wait()
    for h in range(GROUP):
        c = cut(h)
        rate = rate_row(rates, h)
        kv = tn(scaled(pk[:, c], jnp.exp(-rate * (D - 1.0 - rows()))), pv[:, c]).astype(BF16)
        qd = tn(scaled(pq[:, c], jnp.exp(-rate * rows())), pg[:, c]).astype(BF16)
        for k in range(8):
            parts[h, k, 0:PART] = kv[k * PART : (k + 1) * PART]
            parts[h, k, PART : 2 * PART] = qd[k * PART : (k + 1) * PART]
        stores[1 + h].start()
    for store in stores:
        store.wait()


def carried_kernel(lengths, rates, rq, rg, carried, masked):
    for h in range(PAIR):
        rate = rate_row(rates, GROUP + h)
        total = jnp.zeros((D, D), F32)
        for j in range(2):
            inside = lax.broadcasted_iota(jnp.int32, (D, D), 0) + j * D < lengths[0]
            grad = jnp.where(inside, rg[0, cut(j), cut(h)].astype(F32), 0.0).astype(BF16)
            masked[cut(j), cut(h)] = grad
            weight = jnp.exp(-rate * (rows() + float(j * D)))
            total += tn(scaled(rq[0, cut(j), cut(h)], weight), grad)
        carried[8 * h : 8 * h + 8] = total.astype(BF16).reshape(8, PART, D)


def decay_mask(rate):
    offsets = rows() - lax.broadcasted_iota(jnp.int32, (D, D), 1).astype(F32)
    return jnp.where(offsets >= 0.0, jnp.exp(-rate * jnp.maximum(offsets, 0.0)), 0.0)


def local_grads(q, k, v, g, mask):
    weights = (nt(q, k) * mask).astype(BF16)
    dscores = (nt(g, v) * mask).astype(BF16)
    return nn(dscores, k), tn(dscores, q), tn(weights, g)


def local_kernel(rates, pq, pk, pv, pg, pdq, pdk, pdv, w_in, w_out, token):
    token[...] = jnp.zeros_like(token)
    for h in range(GROUP):
        c = cut(h)
        rate = rate_row(rates, h)
        mask = decay_mask(rate)
        w_in[:, c] = jnp.exp(-rate * (rows() + 1.0))
        w_out[:, c] = jnp.exp(-rate * (float(D) - rows()))
        pdq[:, c], pdk[:, c], pdv[:, c] = local_grads(pq[:, c], pk[:, c], pv[:, c], pg[:, c], mask)


def resp_kernel(rates, rq, rk, rv, masked, after, rdq, rdk, rdv, w_resp):
    for h in range(PAIR):
        c = cut(h)
        rate = rate_row(rates, GROUP + h)
        mask = decay_mask(rate)
        g0, g1 = masked[cut(0), c], masked[cut(1), c]
        for j in range(2):
            w_resp[cut(j), c] = jnp.exp(-rate * (rows() + float(j * D + 1)))
        q0, q1 = rq[0, cut(0), c], rq[0, cut(1), c]
        k0, k1 = rk[0, cut(0), c], rk[0, cut(1), c]
        v0, v1 = rv[0, cut(0), c], rv[0, cut(1), c]
        resp_in = tn(scaled(k0, jnp.exp(-rate * (D - 1.0 - rows()))), v0).astype(BF16)
        resp_out = tn(scaled(q1, jnp.exp(-rate * rows())), g1).astype(BF16)
        dq, dk, dv = local_grads(q0, k0, v0, g0, mask)
        out_weight = jnp.exp(-rate * (float(D) - rows()))
        rdq[cut(0), c] = dq
        rdk[0, cut(0), c] = (dk + nt(v0, resp_out) * out_weight).astype(BF16)
        rdv[0, cut(0), c] = (dv + nn(k0, resp_out) * out_weight).astype(BF16)
        dq, dk, dv = local_grads(q1, k1, v1, g1, mask)
        rdq[cut(1), c] = dq + nt(g1, resp_in) * jnp.exp(-rate * (rows() + 1.0))
        rdk[0, cut(1), c] = dk.astype(BF16)
        rdv[0, cut(1), c] = dv.astype(BF16)


def start_kernel(rates, got, carried, before, out):
    decay = rates[48:49]
    state = jnp.zeros((PART, D), F32)
    for b in range(CHAIN):
        state = state * decay + got[b, 0:PART].astype(F32)
    start = state.astype(BF16)
    for j in range(RESPS):
        out[j, 0:PART] = start
        out[j, PART : 2 * PART] = carried[j]


def states_kernel(rates, got, got_two, out, start, token):
    decay = rates[48:49]
    ahead = jnp.zeros((PART, D), F32)
    behind = jnp.zeros((PART, D), F32)
    for j in range(RESPS):
        behind = behind + got_two[j, PART : 2 * PART].astype(F32)
    for b in range(CHAIN):
        out[b, 0:PART] = ahead.astype(BF16)
        ahead = ahead * decay + got[b, 0:PART].astype(F32)
        e = CHAIN - 1 - b
        out[e, PART : 2 * PART] = behind.astype(BF16)
        behind = behind * decay + got[e, PART : 2 * PART].astype(F32)
    for j in range(RESPS):
        start[j] = got_two[j, 0:PART]
    token[...] = jnp.zeros_like(token)


def final_kernel(
    w_in, w_out, w_resp, pk, pv, pg, states, pdq, pdk, pdv, masked, start, start_two, rdq, dq, dk, dv, resp_dq
):
    for h in range(PAIR):
        c = cut(h)
        cuts = slice(8 * h, 8 * h + 8)
        state = (start[cuts] + start_two[cuts]).reshape(D, D)
        for j in range(2):
            weight = w_resp[cut(j), c]
            term = nt(masked[cut(j), c], state) * weight
            resp_dq[0, cut(j), c] = (rdq[cut(j), c] + term).astype(BF16)
    for h in range(GROUP):
        c = cut(h)
        both = [states[owner(h, k)] for k in range(8)]
        state_in = jnp.concatenate([b[0:PART] for b in both], axis=0)
        state_out = jnp.concatenate([b[PART : 2 * PART] for b in both], axis=0)
        weight = w_in[:, c]
        dq[:, c] = (pdq[:, c] + nt(pg[:, c], state_in) * weight).astype(BF16)
        weight = w_out[:, c]
        dk[:, c] = (pdk[:, c] + nt(pv[:, c], state_out) * weight).astype(BF16)
        dv[:, c] = (pdv[:, c] + nn(pk[:, c], state_out) * weight).astype(BF16)


def call(kernel, arrays, outs, flops, in_specs=None, out_specs=None, scratch_shapes=(), limit=8 << 20):
    moved = sum(a.size * a.dtype.itemsize for a in arrays)
    moved += sum(o.size * o.dtype.itemsize for o in outs)
    vmem = pl.BlockSpec(memory_space=pltpu.VMEM)
    got = pl.pallas_call(
        kernel,
        out_shape=tuple(outs),
        in_specs=in_specs or [vmem] * len(arrays),
        out_specs=tuple(out_specs or [vmem] * len(outs)),
        scratch_shapes=scratch_shapes,
        cost_estimate=pl.CostEstimate(flops=flops, bytes_accessed=moved, transcendentals=0),
        compiler_params=pltpu.CompilerParams(vmem_limit_bytes=limit),
        name=kernel.__name__,
    )(*arrays)
    return got if len(outs) > 1 else got[0]


def shaped(shape, dtype):
    return jax.ShapeDtypeStruct(shape, dtype)


def local(there, back, pq, pk, pv, pg, rq, rk, rv, rg, lengths, exps):
    cube = 2 * D * D * D
    flat = (D, GROUP * D)
    token = shaped((8, D), F32)
    slots = shaped((CHAIN, 2 * PART, D), BF16)
    pair = shaped((RESPS, PART, D), BF16)
    resp_out = shaped(rq.shape, BF16)
    cores = [list(range(core, CHAIN, 2)) for core in range(2)]
    hbm = pl.BlockSpec(memory_space=pltpu.HBM)
    rates = shaped((56, D), F32)
    masked = shaped(rq.shape[1:], BF16)
    sources = [pq, pk, pv, pg]
    parts, rates = call(
        parts_kernel,
        [exps] + sources,
        [shaped((PAIR, 8, PAIR, 2 * PART, D), BF16), rates],
        8 * cube,
        [hbm] * 5,
        [hbm] * 2,
        [pltpu.SMEM(exps.shape, exps.dtype)]
        + [pltpu.VMEM(a.shape, a.dtype) for a in sources]
        + [pltpu.VMEM((GROUP, 8, 2 * PART, D), BF16), pltpu.VMEM(rates.shape, F32)]
        + [pltpu.SemaphoreType.DMA((5,)), pltpu.SemaphoreType.DMA((1 + GROUP,))],
        limit=None,
    )
    carried, masked = call(
        carried_kernel,
        [lengths, rates, rq, rg],
        [pair, masked],
        4 * cube,
        [pl.BlockSpec(memory_space=pltpu.SMEM)] + [pl.BlockSpec(memory_space=pltpu.VMEM)] * 3,
    )
    got = lax.all_to_all(parts.reshape(slots.shape), "prefix", 0, 0)
    carried = lax.ppermute(carried, ("prefix", "resp"), there)
    pdq, pdk, pdv, w_in, w_out, before = call(
        local_kernel, [rates, pq, pk, pv, pg], [shaped(flat, F32)] * 5 + [token], 20 * cube
    )
    sent = call(
        start_kernel, [rates, got, carried, before], [shaped((RESPS, 2 * PART, D), BF16)], cube
    )
    got_two = lax.all_to_all(sent, "prefix", 0, 0, axis_index_groups=cores)
    states, start, after = call(
        states_kernel, [rates, got, got_two], [slots, pair, token], cube
    )
    rdq, rdk, rdv, w_resp = call(
        resp_kernel,
        [rates, rq, rk, rv, masked, after],
        [shaped(rq.shape[1:], F32), resp_out, resp_out, shaped(rq.shape[1:], F32)],
        28 * cube,
    )
    states = lax.all_to_all(states, "prefix", 0, 0)
    starts = [lax.ppermute(start, ("prefix", "resp"), pairs) for pairs in back]
    pre_dq, pre_dk, pre_dv, resp_dq = call(
        final_kernel,
        [w_in, w_out, w_resp, pk, pv, pg, states, pdq, pdk, pdv, masked, *starts, rdq],
        [shaped(flat, BF16)] * 3 + [resp_out],
        16 * cube,
    )
    return pre_dq, pre_dk, pre_dv, resp_dq, rdk, rdv


def solution(mesh):
    there = exchange_pairs(GATHER, 0)
    back = [[(b, a) for a, b in exchange_pairs(SPREAD, turn)] for turn in range(2)]
    prompt, response = P("prefix", "resp"), P("resp", None, "prefix")
    return jax.shard_map(
        functools.partial(local, there, back),
        mesh=mesh,
        in_specs=(prompt,) * 4 + (response,) * 4 + (P("resp"), P()),
        out_specs=(prompt,) * 3 + (response,) * 3,
        check_vma=False,
    )
```

```python
import functools

import jax
import jax.numpy as jnp
from jax import lax
from jax.experimental import pallas as pl
from jax.experimental.pallas import tpu as pltpu
from jax.sharding import PartitionSpec as P

D = 128
GROUP = 4
PAIR = 2
CHAIN = 32
RESPS = 16
PART = 16
F32 = jnp.float32
BF16 = jnp.bfloat16


GATHER = (
    "5ca74d96ef013b82",
    "4dfa7ce836b90521",
    "906eb47fa18d235c",
    "ec4fda169b058327",
    "1ac789e60bd23f45",
    "71bf2935e0846acd",
    "d51ac023f79be648",
    "9d82ac135f4b7e60",
    "e813cf274b95da06",
    "6c9035a17df24eb8",
    "23fb15e9046ca7d8",
    "a250c378d14f9b6e",
    "fb5d2c478a6309e1",
    "3ae50bfd296c1847",
    "748c6e9f532d01ab",
    "f64ce758d02a913b",
)
SPREAD = (
    "nvf7hpa2go806e91",
    "goefhpq82b193i0a",
    "80hrb1jpa2iq934c",
    "qd5h43j69b2ica1r",
    "2td5jrb3lae6ksc4",
    "7mfckuabltse645d",
    "f4nuc0tvd7l8e6m5",
    "9dnva81gue0m7f65",
    "oa01ge86hp75df29",
    "hp917oa2igf3bq80",
    "2a9b1jc80hip34rq",
    "b3jra29ed4isc15q",
    "9bcdse45la6krt32",
    "luc64td5fse7mkb3",
    "5fmc6e8d70tu4lnv",
    "e6duf7nv851a90mo",
)


def exchange_pairs(table, turn):
    pairs = []
    for column in range(RESPS):
        for resp in range(RESPS):
            at, chip = divmod(int(table[column][resp], 32), 16)
            if at == turn:
                for core in range(2):
                    response = (2 * column + core) * RESPS + resp
                    pairs.append((response, (2 * chip + core) * RESPS + column))
    return sorted(pairs)


def nt(a, b):
    return lax.dot_general(a, b, (((1,), (1,)), ((), ())), preferred_element_type=F32)


def tn(a, b):
    return lax.dot_general(a, b, (((0,), (0,)), ((), ())), preferred_element_type=F32)


def nn(a, b):
    return lax.dot_general(a, b, (((1,), (0,)), ((), ())), preferred_element_type=F32)


def rate_of(exps_ref, head, shape=(D, D)):
    return jnp.exp2(-jnp.full(shape, exps_ref[head].astype(F32), F32) / 1024.0)


def rate_row(rates, index):
    return rates[8 * index : 8 * index + 1]


def rows(shape=(D, D)):
    return lax.broadcasted_iota(jnp.int32, shape, 0).astype(F32)


def cut(head):
    return slice(head * D, (head + 1) * D)


def scaled(x, weight):
    return (x.astype(F32) * weight).astype(BF16)


def owner(head, part):
    return 2 * (8 * (head % PAIR) + part) + head // PAIR


def parts_kernel(
    exps_in, pq_in, pk_in, pv_in, pg_in, out, rates_out,
    exps, pq, pk, pv, pg, parts, rates, loaded, stored,
):
    def copies(pairs, sems):
        return [pltpu.make_async_copy(a, b, sems.at[i]) for i, (a, b) in enumerate(pairs)]

    loads = copies(
        ((exps_in, exps), (pk_in, pk), (pv_in, pv), (pq_in, pq), (pg_in, pg)), loaded
    )
    stores = copies(
        ((rates, rates_out),)
        + tuple((parts.at[h], out.at[h % PAIR, :, h // PAIR]) for h in range(GROUP)),
        stored,
    )
    for load in loads:
        load.start()
    mine, column = lax.axis_index("prefix"), lax.axis_index("resp")
    heads = [column * GROUP + h for h in range(GROUP)] + [mine * PAIR + h for h in range(PAIR)]
    loads[0].wait()
    for i, head in enumerate(heads):
        rates[8 * i : 8 * i + 8] = rate_of(exps, head, (8, D))
    tract = rate_of(exps, column * GROUP + mine % 2 * PAIR + mine // 16, (8, D))
    rates[48:56] = jnp.exp(-tract * float(D))
    stores[0].start()
    for load in loads[1:]:
        load.wait()
    for h in range(GROUP):
        c = cut(h)
        rate = rate_row(rates, h)
        kv = tn(scaled(pk[:, c], jnp.exp(-rate * (D - 1.0 - rows()))), pv[:, c]).astype(BF16)
        qd = tn(scaled(pq[:, c], jnp.exp(-rate * rows())), pg[:, c]).astype(BF16)
        for k in range(8):
            parts[h, k, 0:PART] = kv[k * PART : (k + 1) * PART]
            parts[h, k, PART : 2 * PART] = qd[k * PART : (k + 1) * PART]
        stores[1 + h].start()
    for store in stores:
        store.wait()


def carried_kernel(lengths, rates, rq, rg, carried, masked):
    for h in range(PAIR):
        rate = rate_row(rates, GROUP + h)
        total = jnp.zeros((D, D), F32)
        for j in range(2):
            inside = lax.broadcasted_iota(jnp.int32, (D, D), 0) + j * D < lengths[0]
            grad = jnp.where(inside, rg[0, cut(j), cut(h)].astype(F32), 0.0).astype(BF16)
            masked[cut(j), cut(h)] = grad
            weight = jnp.exp(-rate * (rows() + float(j * D)))
            total += tn(scaled(rq[0, cut(j), cut(h)], weight), grad)
        carried[8 * h : 8 * h + 8] = total.astype(BF16).reshape(8, PART, D)


def decay_mask(rate):
    offsets = rows() - lax.broadcasted_iota(jnp.int32, (D, D), 1).astype(F32)
    return jnp.where(offsets >= 0.0, jnp.exp(-rate * jnp.maximum(offsets, 0.0)), 0.0)


def local_grads(q, k, v, g, mask):
    weights = (nt(q, k) * mask).astype(BF16)
    dscores = (nt(g, v) * mask).astype(BF16)
    return nn(dscores, k), tn(dscores, q), tn(weights, g)


def local_kernel(rates, pq, pk, pv, pg, pdq, pdk, pdv, token):
    token[...] = jnp.zeros_like(token)
    for h in range(GROUP):
        c = cut(h)
        mask = decay_mask(rate_row(rates, h))
        pdq[:, c], pdk[:, c], pdv[:, c] = local_grads(pq[:, c], pk[:, c], pv[:, c], pg[:, c], mask)


def resp_kernel(rates, rq, rk, rv, masked, after, rdq, rdk, rdv, token):
    token[...] = jnp.zeros_like(token)
    for h in range(PAIR):
        c = cut(h)
        rate = rate_row(rates, GROUP + h)
        mask = decay_mask(rate)
        g0, g1 = masked[cut(0), c], masked[cut(1), c]
        q0, q1 = rq[0, cut(0), c], rq[0, cut(1), c]
        k0, k1 = rk[0, cut(0), c], rk[0, cut(1), c]
        v0, v1 = rv[0, cut(0), c], rv[0, cut(1), c]
        resp_in = tn(scaled(k0, jnp.exp(-rate * (D - 1.0 - rows()))), v0).astype(BF16)
        resp_out = tn(scaled(q1, jnp.exp(-rate * rows())), g1).astype(BF16)
        dq, dk, dv = local_grads(q0, k0, v0, g0, mask)
        out_weight = jnp.exp(-rate * (float(D) - rows()))
        rdq[cut(0), c] = dq
        rdk[0, cut(0), c] = (dk + nt(v0, resp_out) * out_weight).astype(BF16)
        rdv[0, cut(0), c] = (dv + nn(k0, resp_out) * out_weight).astype(BF16)
        dq, dk, dv = local_grads(q1, k1, v1, g1, mask)
        rdq[cut(1), c] = dq + nt(g1, resp_in) * jnp.exp(-rate * (rows() + 1.0))
        rdk[0, cut(1), c] = dk.astype(BF16)
        rdv[0, cut(1), c] = dv.astype(BF16)


def start_kernel(rates, got, carried, before, out):
    decay = rates[48:49]
    state = jnp.zeros((PART, D), F32)
    for b in range(CHAIN):
        state = state * decay + got[b, 0:PART].astype(F32)
    start = state.astype(BF16)
    for j in range(RESPS):
        out[j, 0:PART] = start
        out[j, PART : 2 * PART] = carried[j]


def states_kernel(rates, got, got_two, out, start):
    decay = rates[48:49]
    ahead = jnp.zeros((PART, D), F32)
    behind = jnp.zeros((PART, D), F32)
    for j in range(RESPS):
        behind = behind + got_two[j, PART : 2 * PART].astype(F32)
    for b in range(CHAIN):
        out[b, 0:PART] = ahead.astype(BF16)
        ahead = ahead * decay + got[b, 0:PART].astype(F32)
        e = CHAIN - 1 - b
        out[e, PART : 2 * PART] = behind.astype(BF16)
        behind = behind * decay + got[e, PART : 2 * PART].astype(F32)
    for j in range(RESPS):
        start[j] = got_two[j, 0:PART]


def final_kernel(
    rates, pk, pv, pg, states, pdq, pdk, pdv, masked, start, start_two, rdq, dq, dk, dv, resp_dq
):
    for h in range(PAIR):
        c = cut(h)
        rate = rate_row(rates, GROUP + h)
        cuts = slice(8 * h, 8 * h + 8)
        state = (start[cuts] + start_two[cuts]).reshape(D, D)
        for j in range(2):
            weight = jnp.exp(-rate * (rows() + float(j * D + 1)))
            term = nt(masked[cut(j), c], state) * weight
            resp_dq[0, cut(j), c] = (rdq[cut(j), c] + term).astype(BF16)
    for h in range(GROUP):
        c = cut(h)
        rate = rate_row(rates, h)
        both = [states[owner(h, k)] for k in range(8)]
        state_in = jnp.concatenate([b[0:PART] for b in both], axis=0)
        state_out = jnp.concatenate([b[PART : 2 * PART] for b in both], axis=0)
        weight = jnp.exp(-rate * (rows() + 1.0))
        dq[:, c] = (pdq[:, c] + nt(pg[:, c], state_in) * weight).astype(BF16)
        weight = jnp.exp(-rate * (float(D) - rows()))
        dk[:, c] = (pdk[:, c] + nt(pv[:, c], state_out) * weight).astype(BF16)
        dv[:, c] = (pdv[:, c] + nn(pk[:, c], state_out) * weight).astype(BF16)


def call(kernel, arrays, outs, flops, in_specs=None, out_specs=None, scratch_shapes=(), limit=8 << 20):
    moved = sum(a.size * a.dtype.itemsize for a in arrays)
    moved += sum(o.size * o.dtype.itemsize for o in outs)
    vmem = pl.BlockSpec(memory_space=pltpu.VMEM)
    got = pl.pallas_call(
        kernel,
        out_shape=tuple(outs),
        in_specs=in_specs or [vmem] * len(arrays),
        out_specs=tuple(out_specs or [vmem] * len(outs)),
        scratch_shapes=scratch_shapes,
        cost_estimate=pl.CostEstimate(flops=flops, bytes_accessed=moved, transcendentals=0),
        compiler_params=pltpu.CompilerParams(vmem_limit_bytes=limit),
        name=kernel.__name__,
    )(*arrays)
    return got if len(outs) > 1 else got[0]


def shaped(shape, dtype):
    return jax.ShapeDtypeStruct(shape, dtype)


def local(there, back, pq, pk, pv, pg, rq, rk, rv, rg, lengths, exps):
    cube = 2 * D * D * D
    flat = (D, GROUP * D)
    token = shaped((8, D), F32)
    slots = shaped((CHAIN, 2 * PART, D), BF16)
    pair = shaped((RESPS, PART, D), BF16)
    resp_out = shaped(rq.shape, BF16)
    cores = [list(range(core, CHAIN, 2)) for core in range(2)]
    hbm = pl.BlockSpec(memory_space=pltpu.HBM)
    rates = shaped((56, D), F32)
    masked = shaped(rq.shape[1:], BF16)
    sources = [pq, pk, pv, pg]
    parts, rates = call(
        parts_kernel,
        [exps] + sources,
        [shaped((PAIR, 8, PAIR, 2 * PART, D), BF16), rates],
        8 * cube,
        [hbm] * 5,
        [hbm] * 2,
        [pltpu.SMEM(exps.shape, exps.dtype)]
        + [pltpu.VMEM(a.shape, a.dtype) for a in sources]
        + [pltpu.VMEM((GROUP, 8, 2 * PART, D), BF16), pltpu.VMEM(rates.shape, F32)]
        + [pltpu.SemaphoreType.DMA((5,)), pltpu.SemaphoreType.DMA((1 + GROUP,))],
        limit=None,
    )
    carried, masked = call(
        carried_kernel,
        [lengths, rates, rq, rg],
        [pair, masked],
        4 * cube,
        [pl.BlockSpec(memory_space=pltpu.SMEM)] + [pl.BlockSpec(memory_space=pltpu.VMEM)] * 3,
    )
    got = lax.all_to_all(parts.reshape(slots.shape), "prefix", 0, 0)
    carried = lax.ppermute(carried, ("prefix", "resp"), there)
    pdq, pdk, pdv, before = call(
        local_kernel, [rates, pq, pk, pv, pg], [shaped(flat, F32)] * 3 + [token], 20 * cube
    )
    rdq, rdk, rdv, after = call(
        resp_kernel,
        [rates, rq, rk, rv, masked, before],
        [shaped(rq.shape[1:], F32), resp_out, resp_out, token],
        28 * cube,
    )
    sent = call(
        start_kernel, [rates, got, carried, after], [shaped((RESPS, 2 * PART, D), BF16)], cube
    )
    got_two = lax.all_to_all(sent, "prefix", 0, 0, axis_index_groups=cores)
    states, start = call(states_kernel, [rates, got, got_two], [slots, pair], cube)
    states = lax.all_to_all(states, "prefix", 0, 0)
    starts = [lax.ppermute(start, ("prefix", "resp"), pairs) for pairs in back]
    pre_dq, pre_dk, pre_dv, resp_dq = call(
        final_kernel,
        [rates, pk, pv, pg, states, pdq, pdk, pdv, masked, *starts, rdq],
        [shaped(flat, BF16)] * 3 + [resp_out],
        16 * cube,
    )
    return pre_dq, pre_dk, pre_dv, resp_dq, rdk, rdv


def solution(mesh):
    there = exchange_pairs(GATHER, 0)
    back = [[(b, a) for a, b in exchange_pairs(SPREAD, turn)] for turn in range(2)]
    prompt, response = P("prefix", "resp"), P("resp", None, "prefix")
    return jax.shard_map(
        functools.partial(local, there, back),
        mesh=mesh,
        in_specs=(prompt,) * 4 + (response,) * 4 + (P("resp"), P()),
        out_specs=(prompt,) * 3 + (response,) * 3,
        check_vma=False,
    )
```
